32 devices in a mesh: recv: 8 (over z, x), tm: 4 (over y, core).
Axes of the slice: x: 2, y: 2, z: 4, core: 2. Of those that a mesh axis runs over, the one named last changes fastest.
Arguments:
- record: float32 [128, 4096], P('recv', 'tm')
- source_channels: int32 [16], replicated, may hold values from 0 to 127, as said below
- valid_mask: int32 [128, 4], P('recv', 'tm'), may hold values 0 or 1
Outputs:
- lag_stack: float32 [16, 128, 256], P('tm', 'recv')
The draws below stay inside these ranges and needn't reach their ends.
Inputs may be any that keep to these rules, and one draw needn't show every extreme that they name: `source_channels`: ascending and distinct; source s lies in channels s * 8 to (s + 1) * 8 - 1; the first is channel 0 and the last channel 128 - 1.
All inputs are finite; a program needn't handle non-finite values. No bound on the sum of `valid_mask` on one device may be relied on, other than what follows from the above.
Results may differ from the reference program's by a relative error of at most 0.0001.
Values sent between devices are 32-bit elements; how exact they have to be, the bound alone decides.
No kernel may reach another device: no remote copies, remote signals or barrier semaphores. Data moves between devices by JAX's collectives and lax.ppermute only.
A program may use at most 64 MiB of HBM per device.

```python
import jax
import jax.numpy as jnp
from jax import lax

SEGLEN = 2048
HOP = 1024
NF = 1024
LAGS = 256
SMOOTH = 64
NSRC = 16
R = 128
SEGS = 4
NS = 4096


def draw_record(key, part):
    keys = jax.random.split(key, 6)
    white = jax.random.normal(keys[0], (R, NS), jnp.float32)
    common_weight = 0.7
    coef_one = jax.random.uniform(keys[1], (R, 1), jnp.float32, -0.8, 0.8)
    coef_two = jax.random.uniform(keys[2], (R, 1), jnp.float32, -0.6, 0.6)
    colored = white + coef_one * jnp.roll(white, 1, axis=1) + coef_two * jnp.roll(white, 2, axis=1)
    common = jax.random.normal(keys[3], (NS,), jnp.float32)
    delays = jax.random.randint(keys[4], (R, 1), 0, LAGS // 2)
    positions = (jnp.arange(NS)[None, :] - delays) % NS
    shifted = jnp.take(common, positions)
    levels = jnp.exp(jax.random.uniform(keys[5], (R, NS // HOP), jnp.float32, 0.0, 2.3))
    amplitude = jnp.repeat(levels, HOP, axis=1)
    return amplitude * (colored + common_weight * shifted)


def draw_source_channels(key, part):
    block_size = R // NSRC
    offsets = jax.random.randint(key, (NSRC,), 0, block_size)
    offsets = offsets.at[0].set(0).at[NSRC - 1].set(block_size - 1)
    return (jnp.arange(NSRC) * block_size + offsets).astype(jnp.int32)


def with_ends(values, rng, smallest, top_value):
    longest = values.shape.index(max(values.shape))
    spots = []
    for shift in (0, 1):
        where = [jax.random.randint(jax.random.fold_in(rng, axis), (), 0, length) for axis, length in enumerate(values.shape)]
        where[longest] = (where[longest] + shift) % values.shape[longest]
        spots.append(tuple(where))
    return values.at[spots[0]].set(smallest).at[spots[1]].set(top_value)


def setup_inputs(seed: int = 0) -> dict:
    splits = jax.random.split(jax.random.key(seed), 4)
    record = draw_record(jax.random.fold_in(splits[3], 71), 0)
    source_channels = draw_source_channels(jax.random.fold_in(splits[3], 71), 0)
    valid_mask = with_ends((jax.random.randint(splits[2], (R, SEGS), 0, 4) < 3).astype(jnp.int32), jax.random.fold_in(splits[2], 1), 0, 1)
    return {"record": record, "source_channels": source_channels, "valid_mask": valid_mask}


def reference(record, source_channels, valid_mask):
    chan_count = record.shape[0]
    padded = jnp.concatenate([record, jnp.zeros((chan_count, HOP), record.dtype)], axis=1)
    sample_idx = jnp.arange(SEGLEN)
    taper_weights = 0.5 - 0.5 * jnp.cos(2.0 * jnp.pi * sample_idx.astype(record.dtype) / SEGLEN)
    zero_init = jnp.zeros((), record.dtype)
    counts = lax.reduce_window(jnp.ones((1, NF), record.dtype), zero_init, lax.add, (1, 2 * SMOOTH + 1), (1, 1), [(0, 0), (SMOOTH, SMOOTH)])
    lag_index = (jnp.arange(LAGS) - LAGS // 2) % SEGLEN
    mask_float = valid_mask.astype(jnp.float32)

    def spectra_of(segment_no):
        segment = lax.dynamic_slice_in_dim(padded, segment_no * HOP, SEGLEN, 1)
        segment = (segment - lax.optimization_barrier(jnp.mean(segment, axis=1, keepdims=True))) * taper_weights
        spectrum = jnp.fft.rfft(segment, axis=1)[:, :NF]
        spec_re = jnp.real(spectrum)
        spec_im = jnp.imag(spectrum)
        power_spec = spec_re * spec_re + spec_im * spec_im
        smoothed = lax.reduce_window(power_spec, zero_init, lax.add, (1, 2 * SMOOTH + 1), (1, 1), [(0, 0), (SMOOTH, SMOOTH)]) / counts
        inv_scale = 1.0 / jnp.sqrt(smoothed + 1e-06)
        return (spec_re * inv_scale, spec_im * inv_scale)

    def add_segment(lag_stack, segment_no):
        white_re, white_im = spectra_of(segment_no)
        src_re = white_re[source_channels]
        src_im = white_im[source_channels]
        recv_valid = lax.dynamic_index_in_dim(mask_float, segment_no, 1, keepdims=False)
        src_valid = recv_valid[source_channels]

        def one_source(packed):
            one_re, one_im, one_valid = packed
            cross_re = one_re[None, :] * white_re + one_im[None, :] * white_im
            cross_im = one_re[None, :] * white_im - one_im[None, :] * white_re
            full = jnp.pad(lax.complex(cross_re, cross_im), ((0, 0), (0, 1)))
            lag_corr = jnp.take(jnp.fft.irfft(full, n=SEGLEN, axis=1), lag_index, axis=1)
            normed = lag_corr / jnp.sqrt(lax.optimization_barrier(jnp.mean(lag_corr * lag_corr, axis=1, keepdims=True)) + 1e-06)
            return normed * (one_valid * recv_valid)[:, None]
        return (lag_stack + lax.map(one_source, (src_re, src_im, src_valid)), None)
    start = jnp.zeros((NSRC, chan_count, LAGS), jnp.float32)
    lag_stack, unused = lax.scan(add_segment, start, jnp.arange(SEGS))
    return lag_stack
```

```python
import functools

import jax
import jax.numpy as jnp
import ml_dtypes
import numpy as np
from jax import lax
from jax.experimental import pallas as pl
from jax.experimental.pallas import tpu as pltpu
from jax.sharding import PartitionSpec as P

LANES = 128
LAGS = 256
SMOOTH = 64
RADIX = 16
PAIRS = RADIX // 2
BF = jnp.bfloat16
F32 = jnp.float32


def order():
    return [(0, 8)] + [(p, RADIX - p) for p in range(1, PAIRS)]


def halves(table):
    high = table.astype(ml_dtypes.bfloat16)
    low = (table - high.astype(np.float64)).astype(ml_dtypes.bfloat16)
    return high, low


@functools.cache
def tables(seglen):
    bins = seglen // 2
    keep = bins // RADIX
    samples = np.arange(seglen)
    taper = (0.5 - 0.5 * np.cos(2 * np.pi * samples / seglen)).reshape(RADIX, LANES)
    n2 = np.arange(LANES)[:, None]
    f2 = np.arange(keep)[None, :]
    forward = np.zeros((PAIRS, 2 * LANES, 2 * LANES))
    lag = np.zeros((PAIRS, 2, 2, keep, LAGS))
    counts = np.zeros((PAIRS, 2, 2, keep))
    lags = np.arange(LAGS)[None, :] - LAGS // 2
    for p, pair in enumerate(order()):
        for half, f1 in enumerate(pair):
            angle = 2 * np.pi * ((n2 * (f1 + RADIX * f2)) % seglen) / seglen
            cos, sin = np.cos(angle), np.sin(angle)
            cols = slice(half * LANES, (half + 1) * LANES)
            if p == 0:
                rows = slice(half * LANES, (half + 1) * LANES)
                forward[p, rows, cols] = np.concatenate([cos, -sin], 1)
            else:
                sign = -1.0 if half == 0 else 1.0
                forward[p, :LANES, cols] = np.concatenate([cos, -sin], 1)
                forward[p, LANES:, cols] = sign * np.concatenate([sin, cos], 1)
            f = f1 + RADIX * np.arange(keep)[:, None]
            angle = 2 * np.pi * ((f * lags) % seglen) / seglen
            factor = np.where(f == 0, 1.0, 2.0) / seglen
            lag[p, half, 0] = factor * np.cos(angle)
            lag[p, half, 1] = -factor * np.sin(angle)
            f = f[:, 0]
            counts[p, half] = np.minimum(f + SMOOTH, bins - 1) - np.maximum(f - SMOOTH, 0) + 1
    inverse_counts = (1.0 / counts).reshape(RADIX, LANES)
    lag = lag.reshape(PAIRS, 2 * LANES, LAGS)
    return (
        taper.astype(np.float32),
        inverse_counts.astype(np.float32),
        *halves(forward),
        *halves(lag),
    )


def radix_step(x):
    r = float(np.sqrt(0.5))
    c1 = float(np.cos(np.pi / 8))
    c3 = float(np.cos(3 * np.pi / 8))
    c = [None] + [x[n] + x[16 - n] for n in range(1, 8)]
    s = [None] + [x[n] - x[16 - n] for n in range(1, 8)]
    e = [x[0] + x[8]] + [c[n] + c[8 - n] for n in range(1, 4)] + [c[4]]
    o = [x[0] - x[8]] + [c[n] - c[8 - n] for n in range(1, 4)]
    g = [None] + [s[n] - s[8 - n] for n in range(1, 4)]
    h = [None] + [s[n] + s[8 - n] for n in range(1, 4)] + [s[4]]
    e04 = e[0] + e[4]
    e04m = e[0] - e[4]
    e13 = e[1] + e[3]
    e13m = r * (e[1] - e[3])
    e042 = e04 + e[2]
    g13 = r * (g[1] + g[3])
    o2 = r * o[2]
    h2 = r * h[2]
    re = {
        0: e042 + e13,
        8: e042 - e13,
        4: e04 - e[2],
        2: e04m + e13m,
        6: e04m - e13m,
        1: (o[0] + o2) + (c1 * o[1] + c3 * o[3]),
        7: (o[0] + o2) - (c1 * o[1] + c3 * o[3]),
        3: (o[0] - o2) + (c3 * o[1] - c1 * o[3]),
        5: (o[0] - o2) - (c3 * o[1] - c1 * o[3]),
    }
    im = {
        2: g13 + g[2],
        4: g[1] - g[3],
        6: g13 - g[2],
        1: (h2 + h[4]) + (c3 * h[1] + c1 * h[3]),
        7: (c3 * h[1] + c1 * h[3]) - (h2 + h[4]),
        3: (h2 - h[4]) + (c1 * h[1] - c3 * h[3]),
        5: (c1 * h[1] - c3 * h[3]) - (h2 - h[4]),
    }
    return [(re[0], re[8])] + [(re[p], im[p]) for p in range(1, PAIRS)]


def split(value):
    high = value.astype(BF)
    return high, (value - high.astype(F32)).astype(BF)


def dot(a, b):
    return jnp.dot(a, b, preferred_element_type=F32)


def spectra(xs, count, shift, taper, high_table, low_table, lhs, z):
    seglen = RADIX * LANES
    step = 16

    def group(first):
        x = [xs[first : first + step, n * LANES : (n + 1) * LANES] for n in range(PAIRS)]
        x += [xs[first + shift : first + shift + step, n * LANES : (n + 1) * LANES] for n in range(PAIRS)]
        total = x[0]
        for part in x[1:]:
            total = total + part
        mean = jnp.sum(total, axis=1, keepdims=True) * (1.0 / seglen)
        x = [(x[n] - mean) * taper[n : n + 1, :] for n in range(RADIX)]
        for p, parts in enumerate(radix_step(x)):
            for i, part in enumerate(parts):
                high, low = split(part)
                lhs[p, first : first + step, i * LANES : (i + 1) * LANES] = high
                lhs[p, count + first : count + first + step, i * LANES : (i + 1) * LANES] = low

    for first in range(0, count, step):
        group(first)
    for p in range(PAIRS):
        both = dot(lhs[p], high_table[p])
        z[p] = both[:count] + both[count:] + dot(lhs[p, :count, :], low_table[p])


def whiten(z, first, inverse_counts, put):
    keep = LANES // 2
    lane = lax.broadcasted_iota(jnp.int32, (8, LANES), 1) % keep
    blocks = [z[q // 2, pl.ds(first, 8), (q % 2) * LANES : (q % 2 + 1) * LANES] for q in range(RADIX)]
    place = [f1 for pair in order() for f1 in pair]
    power = [None] * RADIX
    for q, block in enumerate(blocks):
        square = block * block
        power[place[q]] = square + pltpu.roll(square, keep, 1)
    upto = [power[0]]
    for f1 in range(1, RADIX):
        upto.append(upto[-1] + power[f1])
    since = [power[RADIX - 1]]
    for f1 in range(RADIX - 2, -1, -1):
        since.append(since[-1] + power[f1])
    since = since[::-1]
    total = upto[-1]

    def later(value, by):
        return jnp.where(lane < keep - by, pltpu.roll(value, LANES - by, 1), 0.0)

    def earlier(value, by):
        return jnp.where(lane >= by, pltpu.roll(value, by, 1), 0.0)

    reach = SMOOTH // RADIX
    inner = total
    for by in range(1, reach):
        inner = inner + (later(total, by) + earlier(total, by))
    for q, block in enumerate(blocks):
        f1 = place[q]
        window = inner + (earlier(since[f1], reach) + later(upto[f1], reach))
        scale = lax.rsqrt(window * inverse_counts[q : q + 1, :] + 1e-6)
        put(q, block * scale)


def pick_kernel(per_group, src, *refs):
    blocks, out = refs[:-1], refs[-1]
    rows = blocks[0].shape[0]
    group = lax.axis_index("recv")
    me = lax.axis_index("tm")
    for i in range(per_group):
        row = src[group * per_group + i] - group * rows
        for k, block in enumerate(blocks):
            out[pl.ds((me ^ k) * per_group + i, 1), :] = block[pl.ds(row, 1), :]


def receiver_kernel(segs, *refs):
    blocks = refs[:segs]
    taper, inverse_counts, high_table, low_table, out, mask, xs, lhs, z = refs[segs:]
    rows, width = blocks[0].shape
    hop = width - LANES
    me = lax.axis_index("tm")
    for k, block in enumerate(blocks):
        start = pl.multiple_of((me ^ k) * rows, rows)
        xs[pl.ds(start, rows), :] = block[:, :hop]
        mask[pl.ds(start, rows), :] = block[:, hop:]
    xs[segs * rows :, :] = jnp.zeros((rows, hop), F32)
    count = segs * rows
    spectra(xs, count, rows, taper, high_table, low_table, lhs, z)
    for first in range(0, count, 8):

        def put(q, value):
            out[q // 2, pl.ds(first, 8), (q % 2) * LANES : (q % 2 + 1) * LANES] = value

        whiten(z, first, inverse_counts, put)


def stack_kernel(segs, parts, spectrum, mask, *refs):
    pay = refs[:parts]
    taper, inverse_counts, high_table, low_table, high_lag, low_lag, out = refs[parts : parts + 7]
    xs, lhs, z, straight, crossed, prod_high, prod_low = refs[parts + 7 :]
    hop = pay[0].shape[1] - LANES
    keep = LANES // 2
    per_part = pay[0].shape[0] // segs
    sources = per_part * parts
    rows = mask.shape[0] // segs
    group = lax.axis_index("recv")
    for j, part in enumerate(pay):
        slot = (group + j) % parts
        for k in range(segs):
            for i in range(per_part):
                row = k * per_part + i
                xs[pl.ds(k * sources + slot * per_part + i, 1), :] = part[row : row + 1, :]
    xs[segs * sources :, :] = jnp.zeros((sources, hop + LANES), F32)
    count = segs * sources
    spectra(xs, count, sources, taper, high_table, low_table, lhs, z)
    low_half = lax.broadcasted_iota(jnp.int32, (8, LANES), 1) < keep
    for first in range(0, count, 8):

        def put(q, value):
            turned = pltpu.roll(value, keep, 1)
            cols = slice((q % 2) * LANES, (q % 2 + 1) * LANES)
            straight[q // 2, first : first + 8, cols] = jnp.where(low_half, value, turned)
            crossed[q // 2, first : first + 8, cols] = jnp.where(low_half, turned, -value)

        whiten(z, first, inverse_counts, put)
    total = None
    for p in range(PAIRS):
        for half in range(2):
            cols = slice(half * LANES, (half + 1) * LANES)
            for k in range(segs):
                recv = spectrum[p, k * rows : (k + 1) * rows, cols]
                turned = pltpu.roll(recv, keep, 1)
                for s in range(sources):
                    i = k * sources + s
                    cross = straight[p, i : i + 1, cols] * recv + crossed[p, i : i + 1, cols] * turned
                    prod_high[p, i * rows : (i + 1) * rows, cols], prod_low[p, i * rows : (i + 1) * rows, cols] = split(cross)
        part = dot(prod_high[p], high_lag[p]) + dot(prod_low[p], high_lag[p]) + dot(prod_high[p], low_lag[p])
        total = part if total is None else total + part
    scale = lax.rsqrt(jnp.mean(total * total, axis=1, keepdims=True) + 1e-6)
    normed = total * scale
    for s in range(sources):
        stack = None
        for k in range(segs):
            i = k * sources + s
            weight = mask[k * rows : (k + 1) * rows, :] * xs[i : i + 1, hop:]
            weight = jnp.concatenate([weight] * (LAGS // LANES), axis=1)
            term = weight * normed[i * rows : (i + 1) * rows, :]
            stack = term if stack is None else stack + term
        out[s] = stack


def vmem(count):
    return [pl.BlockSpec(memory_space=pltpu.VMEM)] * count


PARAMS = dict(compiler_params=pltpu.CompilerParams(vmem_limit_bytes=32 * 1024 * 1024))


def local(record, source_channels, valid_mask):
    rows, hop = record.shape
    segs = lax.axis_size("tm")
    groups = lax.axis_size("recv")
    sources = source_channels.shape[0]
    mine = sources // segs
    taper, inverse_counts, high_table, low_table, high_lag, low_lag = tables(2 * hop)
    mask = jnp.broadcast_to(valid_mask.astype(F32), (rows, LANES))
    payload = jnp.concatenate([record, mask], axis=1)
    width = hop + LANES
    blocks = [payload] + [lax.ppermute(payload, "tm", [(i, i ^ k) for i in range(segs)]) for k in range(1, segs)]

    if groups <= sources and groups % segs == 0:
        per_group = sources // groups
        parts = groups // segs
        picked = pl.pallas_call(
            functools.partial(pick_kernel, per_group),
            out_shape=jax.ShapeDtypeStruct((segs * per_group, width), F32),
            in_specs=[pl.BlockSpec(memory_space=pltpu.SMEM)] + vmem(segs),
            out_specs=pl.BlockSpec(memory_space=pltpu.VMEM),
            name="pick",
            **PARAMS,
        )(source_channels, *blocks)
        pay = []
        for j in range(parts):
            route = [
                ((t * parts + (r + j) % parts) * segs + (r // parts + segs // 2) % segs, r * segs + t)
                for r in range(groups)
                for t in range(segs)
            ]
            pay.append(lax.ppermute(picked, ("recv", "tm"), route))
    else:
        parts = 1
        row = source_channels - lax.axis_index("recv") * rows
        here = (row >= 0) & (row < rows)
        places = lax.axis_index("tm") ^ jnp.arange(segs)
        held = jnp.stack(blocks)[places]
        picked = jnp.where(here[None, :, None], held[:, jnp.clip(row, 0, rows - 1), :], 0.0)
        whole = lax.psum(picked, "recv")
        whole = lax.dynamic_slice_in_dim(whole, lax.axis_index("tm") * mine, mine, 1)
        pay = [whole.reshape(segs * mine, width)]

    count = segs * rows
    spectrum, weights = pl.pallas_call(
        functools.partial(receiver_kernel, segs),
        out_shape=(
            jax.ShapeDtypeStruct((PAIRS, count, 2 * LANES), F32),
            jax.ShapeDtypeStruct((count, LANES), F32),
        ),
        in_specs=vmem(segs + 4),
        out_specs=tuple(vmem(2)),
        scratch_shapes=[
            pltpu.VMEM((count + rows, hop), F32),
            pltpu.VMEM((PAIRS, 2 * count, 2 * LANES), BF),
            pltpu.VMEM((PAIRS, count, 2 * LANES), F32),
        ],
        name="receivers",
        **PARAMS,
    )(*blocks, taper, inverse_counts, high_table, low_table)

    src_count = segs * mine
    return pl.pallas_call(
        functools.partial(stack_kernel, segs, parts),
        out_shape=jax.ShapeDtypeStruct((mine, rows, LAGS), F32),
        in_specs=vmem(2 + parts + 6),
        out_specs=pl.BlockSpec(memory_space=pltpu.VMEM),
        scratch_shapes=[
            pltpu.VMEM((src_count + mine, width), F32),
            pltpu.VMEM((PAIRS, 2 * src_count, 2 * LANES), BF),
            pltpu.VMEM((PAIRS, src_count, 2 * LANES), F32),
            pltpu.VMEM((PAIRS, src_count, 2 * LANES), F32),
            pltpu.VMEM((PAIRS, src_count, 2 * LANES), F32),
            pltpu.VMEM((PAIRS, src_count * rows, 2 * LANES), BF),
            pltpu.VMEM((PAIRS, src_count * rows, 2 * LANES), BF),
        ],
        name="stacks",
        **PARAMS,
    )(spectrum, weights, *pay, taper, inverse_counts, high_table, low_table, high_lag, low_lag)


def solution(mesh):
    placed = (P("recv", "tm"), P(), P("recv", "tm"))
    return jax.shard_map(
        local, mesh=mesh, in_specs=placed, out_specs=P("tm", "recv", None), check_vma=False
    )
```

```python
import functools

import jax
import jax.numpy as jnp
import ml_dtypes
import numpy as np
from jax import lax
from jax.experimental import pallas as pl
from jax.experimental.pallas import tpu as pltpu
from jax.sharding import PartitionSpec as P

LANES = 128
LAGS = 256
SMOOTH = 64
RADIX = 16
PAIRS = RADIX // 2
BF = jnp.bfloat16
F32 = jnp.float32


def order():
    return [(0, 8)] + [(p, RADIX - p) for p in range(1, PAIRS)]


def halves(table):
    high = table.astype(ml_dtypes.bfloat16)
    return np.stack([high, (table - high.astype(np.float64)).astype(ml_dtypes.bfloat16)])


@functools.cache
def tables(seglen):
    bins = seglen // 2
    keep = bins // RADIX
    samples = np.arange(seglen)
    taper = (0.5 - 0.5 * np.cos(2 * np.pi * samples / seglen)).reshape(RADIX, LANES)
    n2 = np.arange(LANES)[:, None]
    f2 = np.arange(keep)[None, :]
    forward = np.zeros((PAIRS, 2 * LANES, 2 * LANES))
    lag = np.zeros((PAIRS, 2, 2, keep, LAGS))
    counts = np.zeros((PAIRS, 2, 2, keep))
    lags = np.arange(LAGS)[None, :] - LAGS // 2
    for p, pair in enumerate(order()):
        for half, f1 in enumerate(pair):
            angle = 2 * np.pi * ((n2 * (f1 + RADIX * f2)) % seglen) / seglen
            cos, sin = np.cos(angle), np.sin(angle)
            cols = slice(half * LANES, (half + 1) * LANES)
            if p == 0:
                rows = slice(half * LANES, (half + 1) * LANES)
                forward[p, rows, cols] = np.concatenate([cos, -sin], 1)
            else:
                sign = -1.0 if half == 0 else 1.0
                forward[p, :LANES, cols] = np.concatenate([cos, -sin], 1)
                forward[p, LANES:, cols] = sign * np.concatenate([sin, cos], 1)
            f = f1 + RADIX * np.arange(keep)[:, None]
            angle = 2 * np.pi * ((f * lags) % seglen) / seglen
            factor = np.where(f == 0, 1.0, 2.0) / seglen
            lag[p, half, 0] = factor * np.cos(angle)
            lag[p, half, 1] = -factor * np.sin(angle)
            f = f[:, 0]
            counts[p, half] = np.minimum(f + SMOOTH, bins - 1) - np.maximum(f - SMOOTH, 0) + 1
    inverse_counts = (1.0 / counts).reshape(RADIX, LANES)
    lag = lag.reshape(PAIRS, 2 * LANES, LAGS)
    return (
        taper.astype(np.float32),
        inverse_counts.astype(np.float32),
        halves(forward),
        halves(lag),
    )


def radix_step(x):
    r = float(np.sqrt(0.5))
    c1 = float(np.cos(np.pi / 8))
    c3 = float(np.cos(3 * np.pi / 8))
    c = [None] + [x[n] + x[16 - n] for n in range(1, 8)]
    s = [None] + [x[n] - x[16 - n] for n in range(1, 8)]
    e = [x[0] + x[8]] + [c[n] + c[8 - n] for n in range(1, 4)] + [c[4]]
    o = [x[0] - x[8]] + [c[n] - c[8 - n] for n in range(1, 4)]
    g = [None] + [s[n] - s[8 - n] for n in range(1, 4)]
    h = [None] + [s[n] + s[8 - n] for n in range(1, 4)] + [s[4]]
    e04 = e[0] + e[4]
    e04m = e[0] - e[4]
    e13 = e[1] + e[3]
    e13m = r * (e[1] - e[3])
    e042 = e04 + e[2]
    g13 = r * (g[1] + g[3])
    o2 = r * o[2]
    h2 = r * h[2]
    re = {
        0: e042 + e13,
        8: e042 - e13,
        4: e04 - e[2],
        2: e04m + e13m,
        6: e04m - e13m,
        1: (o[0] + o2) + (c1 * o[1] + c3 * o[3]),
        7: (o[0] + o2) - (c1 * o[1] + c3 * o[3]),
        3: (o[0] - o2) + (c3 * o[1] - c1 * o[3]),
        5: (o[0] - o2) - (c3 * o[1] - c1 * o[3]),
    }
    im = {
        2: g13 + g[2],
        4: g[1] - g[3],
        6: g13 - g[2],
        1: (h2 + h[4]) + (c3 * h[1] + c1 * h[3]),
        7: (c3 * h[1] + c1 * h[3]) - (h2 + h[4]),
        3: (h2 - h[4]) + (c1 * h[1] - c3 * h[3]),
        5: (c1 * h[1] - c3 * h[3]) - (h2 - h[4]),
    }
    return [(re[0], re[8])] + [(re[p], im[p]) for p in range(1, PAIRS)]


def split(value):
    high = value.astype(BF)
    return high, (value - high.astype(F32)).astype(BF)


def dot(a, b):
    return jnp.dot(a, b, preferred_element_type=F32)


def spectra(xs, count, shift, taper, table, lhs, z, ready=None):
    seglen = RADIX * LANES
    step = 16

    def group(first):
        x = [xs[first : first + step, n * LANES : (n + 1) * LANES] for n in range(PAIRS)]
        x += [xs[first + shift : first + shift + step, n * LANES : (n + 1) * LANES] for n in range(PAIRS)]
        total = x[0]
        for part in x[1:]:
            total = total + part
        mean = jnp.sum(total, axis=1, keepdims=True) * (1.0 / seglen)
        x = [(x[n] - mean) * taper[n : n + 1, :] for n in range(RADIX)]
        for p, parts in enumerate(radix_step(x)):
            for i, part in enumerate(parts):
                high, low = split(part)
                lhs[p, first : first + step, i * LANES : (i + 1) * LANES] = high
                lhs[p, count + first : count + first + step, i * LANES : (i + 1) * LANES] = low

    for first in range(0, count, step):
        group(first)
    for p in range(PAIRS):
        if ready is not None:
            ready(p)
        both = dot(lhs[p], table[0, p])
        z[p] = both[:count] + both[count:] + dot(lhs[p, :count, :], table[1, p])


def whiten(z, first, inverse_counts, put):
    keep = LANES // 2
    lane = lax.broadcasted_iota(jnp.int32, (8, LANES), 1) % keep
    blocks = [z[q // 2, pl.ds(first, 8), (q % 2) * LANES : (q % 2 + 1) * LANES] for q in range(RADIX)]
    place = [f1 for pair in order() for f1 in pair]
    power = [None] * RADIX
    for q, block in enumerate(blocks):
        square = block * block
        power[place[q]] = square + pltpu.roll(square, keep, 1)
    upto = [power[0]]
    for f1 in range(1, RADIX):
        upto.append(upto[-1] + power[f1])
    since = [power[RADIX - 1]]
    for f1 in range(RADIX - 2, -1, -1):
        since.append(since[-1] + power[f1])
    since = since[::-1]
    total = upto[-1]

    def later(value, by):
        return jnp.where(lane < keep - by, pltpu.roll(value, LANES - by, 1), 0.0)

    def earlier(value, by):
        return jnp.where(lane >= by, pltpu.roll(value, by, 1), 0.0)

    reach = SMOOTH // RADIX
    inner = total
    for by in range(1, reach):
        inner = inner + (later(total, by) + earlier(total, by))
    for q, block in enumerate(blocks):
        f1 = place[q]
        window = inner + (earlier(since[f1], reach) + later(upto[f1], reach))
        scale = lax.rsqrt(window * inverse_counts[q : q + 1, :] + 1e-6)
        put(q, block * scale)


def join_kernel(record, valid, src, out, src_out, row, sems):
    rows, hop = record.shape
    copies = [
        pltpu.make_async_copy(record, out.at[:, pl.ds(0, hop)], sems.at[0]),
        pltpu.make_async_copy(valid, row, sems.at[1]),
        pltpu.make_async_copy(src, src_out, sems.at[2]),
    ]
    for copy in copies:
        copy.start()
    copies[1].wait()
    here = lax.broadcasted_iota(jnp.int32, (rows, rows), 0) == lax.broadcasted_iota(jnp.int32, (rows, rows), 1)
    column = jnp.sum(jnp.where(here, row[...].astype(F32), 0.0), axis=1, keepdims=True)
    out[:, hop:] = jnp.broadcast_to(column, (rows, LANES))
    copies[2].wait()
    copies[0].wait()


def pick_kernel(per_group, src, *refs):
    blocks, out = refs[:-1], refs[-1]
    rows = blocks[0].shape[0]
    group = lax.axis_index("recv")
    me = lax.axis_index("tm")
    for i in range(per_group):
        row = src[group * per_group + i] - group * rows
        for k, block in enumerate(blocks):
            out[pl.ds((me ^ k) * per_group + i, 1), :] = block[pl.ds(row, 1), :]


def receiver_kernel(segs, *refs):
    blocks = refs[:segs]
    constants = refs[segs : segs + 4]
    out, mask, taper, inverse_counts, table, lag, xs, lhs, z, sems = refs[segs + 4 :]
    small = [pltpu.make_async_copy(constants[i], (taper, inverse_counts)[i], sems.at[i]) for i in range(2)]
    steps = [pltpu.make_async_copy(constants[2].at[p // 4, pl.ds(2 * (p % 4), 2)], table.at[p // 4, pl.ds(2 * (p % 4), 2)], sems.at[2 + p]) for p in range(PAIRS)]
    rest = [pltpu.make_async_copy(constants[3].at[p // 4, pl.ds(2 * (p % 4), 2)], lag.at[p // 4, pl.ds(2 * (p % 4), 2)], sems.at[2 + PAIRS + p]) for p in range(PAIRS)]
    for copy in small + steps + rest:
        copy.start()
    rows, width = blocks[0].shape
    hop = width - LANES
    me = lax.axis_index("tm")
    for k, block in enumerate(blocks):
        start = pl.multiple_of((me ^ k) * rows, rows)
        xs[pl.ds(start, rows), :] = block[:, :hop]
        mask[pl.ds(start, rows), :] = block[:, hop:]
    xs[segs * rows :, :] = jnp.zeros((rows, hop), F32)
    count = segs * rows
    for copy in small + steps:
        copy.wait()
    spectra(xs, count, rows, taper, table, lhs, z, None)
    for first in range(0, count, 8):

        def put(q, value):
            out[q // 2, pl.ds(first, 8), (q % 2) * LANES : (q % 2 + 1) * LANES] = value

        whiten(z, first, inverse_counts, put)
    for copy in rest:
        copy.wait()


def stack_kernel(segs, parts, spectrum, mask, *refs):
    pay = refs[:parts]
    taper, inverse_counts, table, lag, out = refs[parts : parts + 5]
    xs, lhs, z, straight, crossed, prod_high, prod_low = refs[parts + 5 :]
    hop = pay[0].shape[1] - LANES
    keep = LANES // 2
    per_part = pay[0].shape[0] // segs
    sources = per_part * parts
    rows = mask.shape[0] // segs
    group = lax.axis_index("recv")
    for j, part in enumerate(pay):
        slot = (group + j) % parts
        for k in range(segs):
            for i in range(per_part):
                row = k * per_part + i
                xs[pl.ds(k * sources + slot * per_part + i, 1), :] = part[row : row + 1, :]
    xs[segs * sources :, :] = jnp.zeros((sources, hop + LANES), F32)
    count = segs * sources
    spectra(xs, count, sources, taper, table, lhs, z)
    low_half = lax.broadcasted_iota(jnp.int32, (8, LANES), 1) < keep
    for first in range(0, count, 8):

        def put(q, value):
            turned = pltpu.roll(value, keep, 1)
            cols = slice((q % 2) * LANES, (q % 2 + 1) * LANES)
            straight[q // 2, first : first + 8, cols] = jnp.where(low_half, value, turned)
            crossed[q // 2, first : first + 8, cols] = jnp.where(low_half, turned, -value)

        whiten(z, first, inverse_counts, put)
    total = None
    for p in range(PAIRS):
        for half in range(2):
            cols = slice(half * LANES, (half + 1) * LANES)
            for k in range(segs):
                recv = spectrum[p, k * rows : (k + 1) * rows, cols]
                turned = pltpu.roll(recv, keep, 1)
                for s in range(sources):
                    i = k * sources + s
                    cross = straight[p, i : i + 1, cols] * recv + crossed[p, i : i + 1, cols] * turned
                    prod_high[p, i * rows : (i + 1) * rows, cols], prod_low[p, i * rows : (i + 1) * rows, cols] = split(cross)
        part = dot(prod_high[p], lag[0, p]) + dot(prod_low[p], lag[0, p]) + dot(prod_high[p], lag[1, p])
        total = part if total is None else total + part
    scale = lax.rsqrt(jnp.mean(total * total, axis=1, keepdims=True) + 1e-6)
    normed = total * scale
    for s in range(sources):
        stack = None
        for k in range(segs):
            i = k * sources + s
            weight = mask[k * rows : (k + 1) * rows, :] * xs[i : i + 1, hop:]
            weight = jnp.concatenate([weight] * (LAGS // LANES), axis=1)
            term = weight * normed[i * rows : (i + 1) * rows, :]
            stack = term if stack is None else stack + term
        out[s] = stack


def vmem(count):
    return [pl.BlockSpec(memory_space=pltpu.VMEM)] * count


PARAMS = dict(compiler_params=pltpu.CompilerParams(vmem_limit_bytes=32 * 1024 * 1024))


def others(value, segs):
    held = {0: value}
    bit = segs // 2
    while bit:
        for k in list(held):
            held[k ^ bit] = lax.ppermute(held[k], "tm", [(i, i ^ bit) for i in range(segs)])
        bit //= 2
    return [held[k] for k in range(segs)]


def local(record, source_channels, valid_mask):
    rows, hop = record.shape
    segs = lax.axis_size("tm")
    groups = lax.axis_size("recv")
    sources = source_channels.shape[0]
    mine = sources // segs
    width = hop + LANES
    constants = [pltpu.with_memory_space_constraint(c, pltpu.HBM) for c in tables(2 * hop)]
    hbm = pl.BlockSpec(memory_space=pltpu.HBM)
    smem = pl.BlockSpec(memory_space=pltpu.SMEM)
    payload, channels = pl.pallas_call(
        join_kernel,
        out_shape=(jax.ShapeDtypeStruct((rows, width), F32), jax.ShapeDtypeStruct((sources,), jnp.int32)),
        in_specs=[hbm] * 3,
        out_specs=tuple(vmem(2)),
        scratch_shapes=[pltpu.VMEM((1, rows), jnp.int32), pltpu.SemaphoreType.DMA((3,))],
        name="join",
        **PARAMS,
    )(
        pltpu.with_memory_space_constraint(record, pltpu.HBM),
        pltpu.with_memory_space_constraint(valid_mask.reshape(1, rows), pltpu.HBM),
        pltpu.with_memory_space_constraint(source_channels, pltpu.HBM),
    )
    blocks = others(payload, segs)

    if groups <= sources and groups % segs == 0:
        per_group = sources // groups
        parts = groups // segs
        picked = pl.pallas_call(
            functools.partial(pick_kernel, per_group),
            out_shape=jax.ShapeDtypeStruct((segs * per_group, width), F32),
            in_specs=[smem] + vmem(segs),
            out_specs=pl.BlockSpec(memory_space=pltpu.VMEM),
            name="pick",
            **PARAMS,
        )(channels, *blocks)
        pay = []
        for j in range(parts):
            route = [
                ((t * parts + (r + j) % parts) * segs + (r // parts + segs // 2) % segs, r * segs + t)
                for r in range(groups)
                for t in range(segs)
            ]
            pay.append(lax.ppermute(picked, ("recv", "tm"), route))
    else:
        parts = 1
        row = source_channels - lax.axis_index("recv") * rows
        here = (row >= 0) & (row < rows)
        places = lax.axis_index("tm") ^ jnp.arange(segs)
        held = jnp.stack(blocks)[places]
        picked = jnp.where(here[None, :, None], held[:, jnp.clip(row, 0, rows - 1), :], 0.0)
        whole = lax.psum(picked, "recv")
        whole = lax.dynamic_slice_in_dim(whole, lax.axis_index("tm") * mine, mine, 1)
        pay = [whole.reshape(segs * mine, width)]

    count = segs * rows
    spectrum, weights, *loaded = pl.pallas_call(
        functools.partial(receiver_kernel, segs),
        out_shape=(
            jax.ShapeDtypeStruct((PAIRS, count, 2 * LANES), F32),
            jax.ShapeDtypeStruct((count, LANES), F32),
            *[jax.ShapeDtypeStruct(c.shape, c.dtype) for c in constants],
        ),
        in_specs=vmem(segs) + [hbm] * len(constants),
        out_specs=tuple(vmem(2 + len(constants))),
        scratch_shapes=[
            pltpu.VMEM((count + rows, hop), F32),
            pltpu.VMEM((PAIRS, 2 * count, 2 * LANES), BF),
            pltpu.VMEM((PAIRS, count, 2 * LANES), F32),
            pltpu.SemaphoreType.DMA((2 + 2 * PAIRS,)),
        ],
        name="receivers",
        **PARAMS,
    )(*blocks, *constants)

    src_count = segs * mine
    return pl.pallas_call(
        functools.partial(stack_kernel, segs, parts),
        out_shape=jax.ShapeDtypeStruct((mine, rows, LAGS), F32),
        in_specs=vmem(2 + parts + 4),
        out_specs=pl.BlockSpec(memory_space=pltpu.VMEM),
        scratch_shapes=[
            pltpu.VMEM((src_count + mine, width), F32),
            pltpu.VMEM((PAIRS, 2 * src_count, 2 * LANES), BF),
            pltpu.VMEM((PAIRS, src_count, 2 * LANES), F32),
            pltpu.VMEM((PAIRS, src_count, 2 * LANES), F32),
            pltpu.VMEM((PAIRS, src_count, 2 * LANES), F32),
            pltpu.VMEM((PAIRS, src_count * rows, 2 * LANES), BF),
            pltpu.VMEM((PAIRS, src_count * rows, 2 * LANES), BF),
        ],
        name="stacks",
        **PARAMS,
    )(spectrum, weights, *pay, *loaded)


def solution(mesh):
    placed = (P("recv", "tm"), P(), P("recv", "tm"))
    return jax.shard_map(
        local, mesh=mesh, in_specs=placed, out_specs=P("tm", "recv", None), check_vma=False
    )
```

```python
import functools

import jax
import jax.numpy as jnp
import ml_dtypes
import numpy as np
from jax import lax
from jax.experimental import pallas as pl
from jax.experimental.pallas import tpu as pltpu
from jax.sharding import PartitionSpec as P

LANES = 128
LAGS = 256
SMOOTH = 64
RADIX = 16
PAIRS = RADIX // 2
BF = jnp.bfloat16
F32 = jnp.float32


def order():
    return [(0, 8)] + [(p, RADIX - p) for p in range(1, PAIRS)]


def halves(table):
    high = table.astype(ml_dtypes.bfloat16)
    return np.stack([high, (table - high.astype(np.float64)).astype(ml_dtypes.bfloat16)])


@functools.cache
def tables(seglen):
    bins = seglen // 2
    keep = bins // RADIX
    samples = np.arange(seglen)
    taper = (0.5 - 0.5 * np.cos(2 * np.pi * samples / seglen)).reshape(RADIX, LANES)
    n2 = np.arange(LANES)[:, None]
    f2 = np.arange(keep)[None, :]
    forward = np.zeros((PAIRS, 2 * LANES, 2 * LANES))
    lag = np.zeros((PAIRS, 2, 2, keep, LAGS))
    counts = np.zeros((PAIRS, 2, 2, keep))
    lags = np.arange(LAGS)[None, :] - LAGS // 2
    for p, pair in enumerate(order()):
        for half, f1 in enumerate(pair):
            angle = 2 * np.pi * ((n2 * (f1 + RADIX * f2)) % seglen) / seglen
            cos, sin = np.cos(angle), np.sin(angle)
            cols = slice(half * LANES, (half + 1) * LANES)
            if p == 0:
                rows = slice(half * LANES, (half + 1) * LANES)
                forward[p, rows, cols] = np.concatenate([cos, -sin], 1)
            else:
                sign = -1.0 if half == 0 else 1.0
                forward[p, :LANES, cols] = np.concatenate([cos, -sin], 1)
                forward[p, LANES:, cols] = sign * np.concatenate([sin, cos], 1)
            f = f1 + RADIX * np.arange(keep)[:, None]
            angle = 2 * np.pi * ((f * lags) % seglen) / seglen
            factor = np.where(f == 0, 1.0, 2.0) / seglen
            lag[p, half, 0] = factor * np.cos(angle)
            lag[p, half, 1] = -factor * np.sin(angle)
            f = f[:, 0]
            counts[p, half] = np.minimum(f + SMOOTH, bins - 1) - np.maximum(f - SMOOTH, 0) + 1
    inverse_counts = (1.0 / counts).reshape(RADIX, LANES)
    lag = lag.reshape(PAIRS, 2 * LANES, LAGS)
    return (
        taper.astype(np.float32),
        inverse_counts.astype(np.float32),
        halves(forward),
        halves(lag),
    )


def radix_step(x):
    r = float(np.sqrt(0.5))
    c1 = float(np.cos(np.pi / 8))
    c3 = float(np.cos(3 * np.pi / 8))
    c = [None] + [x[n] + x[16 - n] for n in range(1, 8)]
    s = [None] + [x[n] - x[16 - n] for n in range(1, 8)]
    e = [x[0] + x[8]] + [c[n] + c[8 - n] for n in range(1, 4)] + [c[4]]
    o = [x[0] - x[8]] + [c[n] - c[8 - n] for n in range(1, 4)]
    g = [None] + [s[n] - s[8 - n] for n in range(1, 4)]
    h = [None] + [s[n] + s[8 - n] for n in range(1, 4)] + [s[4]]
    e04 = e[0] + e[4]
    e04m = e[0] - e[4]
    e13 = e[1] + e[3]
    e13m = r * (e[1] - e[3])
    e042 = e04 + e[2]
    g13 = r * (g[1] + g[3])
    o2 = r * o[2]
    h2 = r * h[2]
    re = {
        0: e042 + e13,
        8: e042 - e13,
        4: e04 - e[2],
        2: e04m + e13m,
        6: e04m - e13m,
        1: (o[0] + o2) + (c1 * o[1] + c3 * o[3]),
        7: (o[0] + o2) - (c1 * o[1] + c3 * o[3]),
        3: (o[0] - o2) + (c3 * o[1] - c1 * o[3]),
        5: (o[0] - o2) - (c3 * o[1] - c1 * o[3]),
    }
    im = {
        2: g13 + g[2],
        4: g[1] - g[3],
        6: g13 - g[2],
        1: (h2 + h[4]) + (c3 * h[1] + c1 * h[3]),
        7: (c3 * h[1] + c1 * h[3]) - (h2 + h[4]),
        3: (h2 - h[4]) + (c1 * h[1] - c3 * h[3]),
        5: (c1 * h[1] - c3 * h[3]) - (h2 - h[4]),
    }
    return [(re[0], re[8])] + [(re[p], im[p]) for p in range(1, PAIRS)]


def split(value):
    high = value.astype(BF)
    return high, (value - high.astype(F32)).astype(BF)


def dot(a, b):
    return jnp.dot(a, b, preferred_element_type=F32)


def spectra(xs, count, shift, taper, table, lhs, z, ready=None):
    seglen = RADIX * LANES
    step = 16

    def group(first):
        x = [xs[first : first + step, n * LANES : (n + 1) * LANES] for n in range(PAIRS)]
        x += [xs[first + shift : first + shift + step, n * LANES : (n + 1) * LANES] for n in range(PAIRS)]
        total = x[0]
        for part in x[1:]:
            total = total + part
        mean = jnp.sum(total, axis=1, keepdims=True) * (1.0 / seglen)
        x = [(x[n] - mean) * taper[n : n + 1, :] for n in range(RADIX)]
        for p, parts in enumerate(radix_step(x)):
            for i, part in enumerate(parts):
                high, low = split(part)
                lhs[p, first : first + step, i * LANES : (i + 1) * LANES] = high
                lhs[p, count + first : count + first + step, i * LANES : (i + 1) * LANES] = low

    for first in range(0, count, step):
        group(first)
    for p in range(PAIRS):
        if ready is not None:
            ready(p)
        both = dot(lhs[p], table[0, p])
        z[p] = both[:count] + both[count:] + dot(lhs[p, :count, :], table[1, p])


def whiten(z, first, inverse_counts, put):
    keep = LANES // 2
    lane = lax.broadcasted_iota(jnp.int32, (8, LANES), 1) % keep
    blocks = [z[q // 2, pl.ds(first, 8), (q % 2) * LANES : (q % 2 + 1) * LANES] for q in range(RADIX)]
    place = [f1 for pair in order() for f1 in pair]
    power = [None] * RADIX
    for q, block in enumerate(blocks):
        square = block * block
        power[place[q]] = square + pltpu.roll(square, keep, 1)
    upto = [power[0]]
    for f1 in range(1, RADIX):
        upto.append(upto[-1] + power[f1])
    since = [power[RADIX - 1]]
    for f1 in range(RADIX - 2, -1, -1):
        since.append(since[-1] + power[f1])
    since = since[::-1]
    total = upto[-1]

    def later(value, by):
        return jnp.where(lane < keep - by, pltpu.roll(value, LANES - by, 1), 0.0)

    def earlier(value, by):
        return jnp.where(lane >= by, pltpu.roll(value, by, 1), 0.0)

    reach = SMOOTH // RADIX
    inner = total
    for by in range(1, reach):
        inner = inner + (later(total, by) + earlier(total, by))
    for q, block in enumerate(blocks):
        f1 = place[q]
        window = inner + (earlier(since[f1], reach) + later(upto[f1], reach))
        scale = lax.rsqrt(window * inverse_counts[q : q + 1, :] + 1e-6)
        put(q, block * scale)


def join_kernel(per_group, record, valid, src, out, *refs):
    *picked, row, channels, sems = refs
    rows, hop = record.shape
    copies = [
        pltpu.make_async_copy(src, channels, sems.at[0]),
        pltpu.make_async_copy(valid, row, sems.at[1]),
        pltpu.make_async_copy(record, out.at[:, pl.ds(0, hop)], sems.at[2]),
    ]
    for copy in copies:
        copy.start()
    copies[1].wait()
    square = (rows, rows)
    here = lax.broadcasted_iota(jnp.int32, square, 0) == lax.broadcasted_iota(jnp.int32, square, 1)
    column = jnp.sum(jnp.where(here, row[...].astype(F32), 0.0), axis=1, keepdims=True)
    out[:, hop:] = jnp.broadcast_to(column, (rows, LANES))
    copies[0].wait()
    copies[2].wait()
    first = lax.axis_index("recv")
    for i in range(per_group):
        place = channels[first * per_group + i] - first * rows
        picked[0][i : i + 1, :] = out[pl.ds(place, 1), :]


def receiver_kernel(segs, *refs):
    blocks = refs[:segs]
    constants = refs[segs : segs + 4]
    out, mask, taper, inverse_counts, table, lag, xs, lhs, z, sems = refs[segs + 4 :]
    small = [pltpu.make_async_copy(constants[i], (taper, inverse_counts)[i], sems.at[i]) for i in range(2)]
    steps = [pltpu.make_async_copy(constants[2].at[p // 4, pl.ds(2 * (p % 4), 2)], table.at[p // 4, pl.ds(2 * (p % 4), 2)], sems.at[2 + p]) for p in range(PAIRS)]
    rest = [pltpu.make_async_copy(constants[3].at[p // 4, pl.ds(2 * (p % 4), 2)], lag.at[p // 4, pl.ds(2 * (p % 4), 2)], sems.at[2 + PAIRS + p]) for p in range(PAIRS)]
    for copy in small + steps + rest:
        copy.start()
    rows, width = blocks[0].shape
    hop = width - LANES
    me = lax.axis_index("tm")
    for k, block in enumerate(blocks):
        start = pl.multiple_of((me ^ k) * rows, rows)
        xs[pl.ds(start, rows), :] = block[:, :hop]
        mask[pl.ds(start, rows), :] = block[:, hop:]
    xs[segs * rows :, :] = jnp.zeros((rows, hop), F32)
    count = segs * rows
    for copy in small + steps:
        copy.wait()
    spectra(xs, count, rows, taper, table, lhs, z, None)
    for first in range(0, count, 8):

        def put(q, value):
            out[q // 2, pl.ds(first, 8), (q % 2) * LANES : (q % 2 + 1) * LANES] = value

        whiten(z, first, inverse_counts, put)
    for copy in rest:
        copy.wait()


def stack_kernel(segs, hops, spectrum, mask, *refs):
    pay = refs[: len(hops)]
    taper, inverse_counts, table, lag, out = refs[len(hops) : len(hops) + 5]
    xs, lhs, z, straight, crossed, prod_high, prod_low = refs[len(hops) + 5 :]
    hop = pay[0].shape[1] - LANES
    keep = LANES // 2
    rows = mask.shape[0] // segs
    group = lax.axis_index("recv")
    me = lax.axis_index("tm")
    parts = 1 + max(turn for turn, _ in hops)
    sources = sum(p.shape[0] for p in pay) // segs
    per_part = sources // parts
    for (turn, pair), part in zip(hops, pay, strict=True):
        slot = (group + turn) % parts
        sender = 0 if pair is None else holder(turn, pair, group // parts, me, segs)
        for k in range(part.shape[0] // per_part):
            for i in range(per_part):
                row = k * per_part + i
                xs[pl.ds((sender ^ k) * sources + slot * per_part + i, 1), :] = part[row : row + 1, :]
    xs[segs * sources :, :] = jnp.zeros((sources, hop + LANES), F32)
    count = segs * sources
    spectra(xs, count, sources, taper, table, lhs, z)
    low_half = lax.broadcasted_iota(jnp.int32, (8, LANES), 1) < keep
    for first in range(0, count, 8):

        def put(q, value):
            turned = pltpu.roll(value, keep, 1)
            cols = slice((q % 2) * LANES, (q % 2 + 1) * LANES)
            straight[q // 2, first : first + 8, cols] = jnp.where(low_half, value, turned)
            crossed[q // 2, first : first + 8, cols] = jnp.where(low_half, turned, -value)

        whiten(z, first, inverse_counts, put)
    total = None
    for p in range(PAIRS):
        for half in range(2):
            cols = slice(half * LANES, (half + 1) * LANES)
            for k in range(segs):
                recv = spectrum[p, k * rows : (k + 1) * rows, cols]
                turned = pltpu.roll(recv, keep, 1)
                for s in range(sources):
                    i = k * sources + s
                    cross = straight[p, i : i + 1, cols] * recv + crossed[p, i : i + 1, cols] * turned
                    prod_high[p, i * rows : (i + 1) * rows, cols], prod_low[p, i * rows : (i + 1) * rows, cols] = split(cross)
        part = dot(prod_high[p], lag[0, p]) + dot(prod_low[p], lag[0, p]) + dot(prod_high[p], lag[1, p])
        total = part if total is None else total + part
    scale = lax.rsqrt(jnp.mean(total * total, axis=1, keepdims=True) + 1e-6)
    for s in range(sources):
        stack = None
        for k in range(segs):
            i = k * sources + s
            weight = mask[k * rows : (k + 1) * rows, 0:1] * xs[i : i + 1, hop : hop + 1]
            term = total[i * rows : (i + 1) * rows, :] * (weight * scale[i * rows : (i + 1) * rows, :])
            stack = term if stack is None else stack + term
        out[s] = stack


def chosen(values, index):
    if isinstance(index, int):
        return values[index]
    return sum(jnp.where(index == i, value, 0) for i, value in enumerate(values))


def holder(turn, pair, place, me, segs):
    if segs != 4 or turn > 1:
        return place ^ (2 * pair)
    base = ((2, 3, 2, 1), (3, 1, 1, 0))[turn]
    flip = ((3, 2, 3, 3), (2, 3, 2, 2))[turn]
    start = (place % 2) * 2 + place // 2 if turn else place
    return start ^ chosen(base, me) ^ (chosen(flip, me) if pair else 0)


def vmem(count):
    return [pl.BlockSpec(memory_space=pltpu.VMEM)] * count


PARAMS = dict(compiler_params=pltpu.CompilerParams(vmem_limit_bytes=32 * 1024 * 1024))


def other(value, segs, k):
    return lax.ppermute(value, "tm", [(i, i ^ k) for i in range(segs)])


def local(record, source_channels, valid_mask):
    rows, hop = record.shape
    segs = lax.axis_size("tm")
    groups = lax.axis_size("recv")
    sources = source_channels.shape[0]
    mine = sources // segs
    width = hop + LANES
    constants = [pltpu.with_memory_space_constraint(c, pltpu.HBM) for c in tables(2 * hop)]
    hbm = pl.BlockSpec(memory_space=pltpu.HBM)
    fast = groups <= sources and groups % segs == 0
    per_group = sources // groups if fast else 0
    payload, *piece = pl.pallas_call(
        functools.partial(join_kernel, per_group),
        out_shape=tuple(jax.ShapeDtypeStruct((n, width), F32) for n in (rows, per_group) if n),
        in_specs=[hbm] * 3,
        out_specs=tuple(vmem(2 if fast else 1)),
        scratch_shapes=[
            pltpu.VMEM((1, rows), jnp.int32),
            pltpu.SMEM((sources,), jnp.int32),
            pltpu.SemaphoreType.DMA((3,)),
        ],
        name="join",
        **PARAMS,
    )(*[pltpu.with_memory_space_constraint(a, pltpu.HBM) for a in (record, valid_mask.reshape(1, rows), source_channels)])
    blocks = [payload] + [other(payload, segs, k) for k in range(1, segs)]
    if fast:
        parts = groups // segs
        picked = jnp.concatenate([piece[0], other(piece[0], segs, 1)], axis=0)
        hops = [(turn, pair) for turn in reversed(range(parts)) for pair in range(segs // 2)]
        pay = []
        for turn, pair in hops:
            route = [
                ((t * parts + (r + turn) % parts) * segs + holder(turn, pair, r // parts, t, segs), r * segs + t)
                for r in range(groups)
                for t in range(segs)
            ]
            pay.append(lax.ppermute(picked, ("recv", "tm"), route))
    else:
        hops = [(0, None)]
        row = source_channels - lax.axis_index("recv") * rows
        here = (row >= 0) & (row < rows)
        mine_now = jnp.where(here[:, None], payload[jnp.clip(row, 0, rows - 1)], 0.0)
        whole = lax.psum(mine_now, "recv").reshape(segs, mine, width)
        whole = lax.all_to_all(whole, "tm", 0, 0)
        pay = [whole.reshape(segs * mine, width)]

    count = segs * rows
    spectrum, weights, *loaded = pl.pallas_call(
        functools.partial(receiver_kernel, segs),
        out_shape=(
            jax.ShapeDtypeStruct((PAIRS, count, 2 * LANES), F32),
            jax.ShapeDtypeStruct((count, LANES), F32),
            *[jax.ShapeDtypeStruct(c.shape, c.dtype) for c in constants],
        ),
        in_specs=vmem(segs) + [hbm] * len(constants),
        out_specs=tuple(vmem(2 + len(constants))),
        scratch_shapes=[
            pltpu.VMEM((count + rows, hop), F32),
            pltpu.VMEM((PAIRS, 2 * count, 2 * LANES), BF),
            pltpu.VMEM((PAIRS, count, 2 * LANES), F32),
            pltpu.SemaphoreType.DMA((2 + 2 * PAIRS,)),
        ],
        name="receivers",
        **PARAMS,
    )(*blocks, *constants)

    src_count = segs * mine
    return pl.pallas_call(
        functools.partial(stack_kernel, segs, hops),
        out_shape=jax.ShapeDtypeStruct((mine, rows, LAGS), F32),
        in_specs=vmem(2 + len(pay) + 4),
        out_specs=pl.BlockSpec(memory_space=pltpu.VMEM),
        scratch_shapes=[
            pltpu.VMEM((src_count + mine, width), F32),
            pltpu.VMEM((PAIRS, 2 * src_count, 2 * LANES), BF),
            pltpu.VMEM((PAIRS, src_count, 2 * LANES), F32),
            pltpu.VMEM((PAIRS, src_count, 2 * LANES), F32),
            pltpu.VMEM((PAIRS, src_count, 2 * LANES), F32),
            pltpu.VMEM((PAIRS, src_count * rows, 2 * LANES), BF),
            pltpu.VMEM((PAIRS, src_count * rows, 2 * LANES), BF),
        ],
        name="stacks",
        **PARAMS,
    )(spectrum, weights, *pay, *loaded)


def solution(mesh):
    placed = (P("recv", "tm"), P(), P("recv", "tm"))
    return jax.shard_map(
        local, mesh=mesh, in_specs=placed, out_specs=P("tm", "recv", None), check_vma=False
    )
```

```python
import functools

import jax
import jax.numpy as jnp
import ml_dtypes
import numpy as np
from jax import lax
from jax.experimental import pallas as pl
from jax.experimental.pallas import tpu as pltpu
from jax.sharding import PartitionSpec as P

LANES = 128
LAGS = 256
SMOOTH = 64
RADIX = 16
PAIRS = RADIX // 2
ROUTES = ((16418906, 3916122, 644028, 12946108), (2217278, 9243262, 12455114, 7848848))
BF = jnp.bfloat16
F32 = jnp.float32


def order():
    return np.arange(PAIRS)[:, None] + PAIRS * np.arange(2)


def halves(table):
    high = table.astype(ml_dtypes.bfloat16)
    return np.stack([high, (table - high.astype(np.float64)).astype(ml_dtypes.bfloat16)])


@functools.cache
def tables(seglen):
    bins = seglen // 2
    keep = bins // RADIX
    samples = np.arange(seglen)
    taper = (0.5 - 0.5 * np.cos(2 * np.pi * samples / seglen)).reshape(RADIX, LANES)
    n2 = np.arange(LANES)[:, None]
    angle = 2 * np.pi * ((n2 * np.arange(keep)[None, :]) % LANES) / LANES
    cos, sin = np.cos(angle), np.sin(angle)
    step = np.concatenate(list(halves(np.block([[cos, -sin], [-sin, -cos]]))), axis=1)
    angle = 2 * np.pi * (np.arange(RADIX)[:, None] * n2.T) / seglen
    f = order()[:, :, None] + RADIX * np.arange(keep)
    counts = np.minimum(f + SMOOTH, bins - 1) - np.maximum(f - SMOOTH, 0) + 1
    inverse_counts = (1.0 / counts).reshape(PAIRS, LANES)
    f2 = np.arange(keep)[:, None]
    angle_low = 2 * np.pi * ((f2 * np.arange(LANES)) % LANES) / LANES
    lags = np.arange(LAGS) - LAGS // 2
    angle_high = 2 * np.pi * np.arange(RADIX)[:, None] * lags / seglen
    factor = 2.0 / seglen
    small = [
        taper,
        np.cos(angle),
        np.sin(angle),
        inverse_counts,
        np.cos(angle_low),
        np.sin(angle_low),
        factor * np.cos(angle_high).reshape(-1, LANES),
        factor * np.sin(angle_high).reshape(-1, LANES),
    ]
    return np.concatenate(small).astype(np.float32), step


def radix_step(x):
    r = float(np.sqrt(0.5))
    c1 = float(np.cos(np.pi / 8))
    c3 = float(np.cos(3 * np.pi / 8))
    c = [None] + [x[n] + x[16 - n] for n in range(1, 8)]
    s = [None] + [x[n] - x[16 - n] for n in range(1, 8)]
    e = [x[0] + x[8]] + [c[n] + c[8 - n] for n in range(1, 4)] + [c[4]]
    o = [x[0] - x[8]] + [c[n] - c[8 - n] for n in range(1, 4)]
    g = [None] + [s[n] - s[8 - n] for n in range(1, 4)]
    h = [None] + [s[n] + s[8 - n] for n in range(1, 4)] + [s[4]]
    e04 = e[0] + e[4]
    e04m = e[0] - e[4]
    e13 = e[1] + e[3]
    e13m = r * (e[1] - e[3])
    e042 = e04 + e[2]
    g13 = r * (g[1] + g[3])
    o2 = r * o[2]
    h2 = r * h[2]
    re = {
        0: e042 + e13,
        8: e042 - e13,
        4: e04 - e[2],
        2: e04m + e13m,
        6: e04m - e13m,
        1: (o[0] + o2) + (c1 * o[1] + c3 * o[3]),
        7: (o[0] + o2) - (c1 * o[1] + c3 * o[3]),
        3: (o[0] - o2) + (c3 * o[1] - c1 * o[3]),
        5: (o[0] - o2) - (c3 * o[1] - c1 * o[3]),
    }
    im = {
        2: g13 + g[2],
        4: g[1] - g[3],
        6: g13 - g[2],
        1: (h2 + h[4]) + (c3 * h[1] + c1 * h[3]),
        7: (c3 * h[1] + c1 * h[3]) - (h2 + h[4]),
        3: (h2 - h[4]) + (c1 * h[1] - c3 * h[3]),
        5: (c1 * h[1] - c3 * h[3]) - (h2 - h[4]),
    }
    return re, im


def split(value):
    high = value.astype(BF)
    return high, (value - high.astype(F32)).astype(BF)


def dot(a, b):
    return jnp.dot(a, b, preferred_element_type=F32)


def spectra(xs, count, shift, small, step_table, lhs, z):
    seglen = RADIX * LANES
    step = 16
    every = RADIX * count

    def group(first):
        x = [xs[first : first + step, n * LANES : (n + 1) * LANES] for n in range(PAIRS)]
        x += [xs[first + shift : first + shift + step, n * LANES : (n + 1) * LANES] for n in range(PAIRS)]
        total = x[0]
        for part in x[1:]:
            total = total + part
        mean = jnp.sum(total, axis=1, keepdims=True) * (1.0 / seglen)
        x = [(x[n] - mean) * small[n : n + 1, :] for n in range(RADIX)]
        re, im = radix_step(x)
        for p in range(PAIRS):
            for half in range(2):
                f1 = p + PAIRS * half
                cos, sin = small[RADIX + f1 : RADIX + f1 + 1, :], small[2 * RADIX + f1 : 2 * RADIX + f1 + 1, :]
                if f1 == 0:
                    parts = (re[0], jnp.zeros_like(re[0]))
                elif f1 == PAIRS:
                    parts = (re[f1] * cos, re[f1] * sin)
                elif f1 < PAIRS:
                    parts = (re[f1] * cos - im[f1] * sin, re[f1] * sin + im[f1] * cos)
                else:
                    a, b = re[RADIX - f1], im[RADIX - f1]
                    parts = (a * cos + b * sin, a * sin - b * cos)
                for i, part in enumerate(parts):
                    high, low = split(part)
                    cols = slice(i * LANES, (i + 1) * LANES)
                    at = f1 * count + first
                    lhs[at : at + step, cols] = high
                    lhs[every + at : every + at + step, cols] = low

    for first in range(0, count, step):
        group(first)
    both = dot(lhs[...], step_table[...])
    both = both[:, :LANES] + both[:, LANES:]
    z[...] = both[:every] + both[every:]


def whiten(z, count, first, small, put):
    keep = LANES // 2
    lane = lax.broadcasted_iota(jnp.int32, (8, LANES), 1)
    place = lane % keep
    upper = lane >= keep
    blocks = []
    for p in range(PAIRS):
        a = z[p * count + first : p * count + first + 8, :]
        b = z[(p + PAIRS) * count + first : (p + PAIRS) * count + first + 8, :]
        blocks.append((jnp.where(upper, pltpu.roll(b, keep, 1), a), jnp.where(upper, b, pltpu.roll(a, keep, 1))))
    power = [x * x + y * y for x, y in blocks]
    upto = [power[0]]
    for p in range(1, PAIRS):
        upto.append(upto[-1] + power[p])
    since = [power[PAIRS - 1]]
    for p in range(PAIRS - 2, -1, -1):
        since.append(since[-1] + power[p])
    since = since[::-1]
    turned = pltpu.roll(upto[-1], keep, 1)
    total = upto[-1] + turned
    below = jnp.where(upper, turned, 0.0)
    above = jnp.where(upper, 0.0, turned)

    def later(value, by):
        return jnp.where(place < keep - by, pltpu.roll(value, LANES - by, 1), 0.0)

    def earlier(value, by):
        return jnp.where(place >= by, pltpu.roll(value, by, 1), 0.0)

    reach = SMOOTH // RADIX
    inner = total
    for by in range(1, reach):
        inner = inner + (later(total, by) + earlier(total, by))
    for p, (x, y) in enumerate(blocks):
        window = inner + (earlier(since[p] + above, reach) + later(upto[p] + below, reach))
        scale = lax.rsqrt(window * small[3 * RADIX + p : 3 * RADIX + p + 1, :] + 1e-6)
        put(p, x * scale, y * scale)


def join_kernel(per_group, record, valid, src, constant, step_constant, out, small, step_table, *refs):
    *picked, row, channels, sems = refs
    rows, hop = record.shape
    copies = [
        pltpu.make_async_copy(src, channels, sems.at[0]),
        pltpu.make_async_copy(valid, row, sems.at[1]),
        pltpu.make_async_copy(record, out.at[:, pl.ds(0, hop)], sems.at[2]),
        pltpu.make_async_copy(constant, small, sems.at[3]),
        pltpu.make_async_copy(step_constant, step_table, sems.at[4]),
    ]
    for copy in copies:
        copy.start()
    copies[1].wait()
    square = (rows, rows)
    here = lax.broadcasted_iota(jnp.int32, square, 0) == lax.broadcasted_iota(jnp.int32, square, 1)
    column = jnp.sum(jnp.where(here, row[...].astype(F32), 0.0), axis=1, keepdims=True)
    out[:, hop:] = jnp.broadcast_to(column, (rows, LANES))
    copies[0].wait()
    copies[2].wait()
    first = lax.axis_index("recv")
    for i in range(per_group):
        place = channels[first * per_group + i] - first * rows
        picked[0][i : i + 1, :] = out[pl.ds(place, 1), :]
    copies[3].wait()
    copies[4].wait()


def lag_kernel(small, lag):
    keep = LANES // 2
    step = 16
    low = 3 * RADIX + PAIRS
    high = low + 2 * keep
    wide = LAGS // LANES
    first = lax.broadcasted_iota(jnp.int32, (step, LANES), 0) == 0
    for f1 in range(RADIX):
        for h in range(wide):
            at = high + f1 * wide + h
            cos_high = small[at : at + 1, :]
            sin_high = small[at + RADIX * wide : at + RADIX * wide + 1, :]
            for f2 in range(0, keep, step):
                cos_low = small[low + f2 : low + f2 + step, :]
                sin_low = small[low + keep + f2 : low + keep + f2 + step, :]
                cos = cos_high * cos_low - sin_high * sin_low
                sin = sin_high * cos_low + cos_high * sin_low
                if f1 == 0 and f2 == 0:
                    cos = jnp.where(first, 0.5 * cos, cos)
                    sin = jnp.where(first, 0.5 * sin, sin)
                for c, value in enumerate((cos, -sin)):
                    row = (2 * (f1 % PAIRS) + c) * LANES + (f1 // PAIRS) * keep + f2
                    for i, part in enumerate(split(value)):
                        lag[i, row : row + step, h * LANES : (h + 1) * LANES] = part


def receiver_kernel(segs, *refs):
    blocks = refs[:segs]
    small, step_table, out, mask, xs, lhs, z = refs[segs:]
    rows, width = blocks[0].shape
    hop = width - LANES
    me = lax.axis_index("tm")
    for k, block in enumerate(blocks):
        start = pl.multiple_of((me ^ k) * rows, rows)
        xs[pl.ds(start, rows), :] = block[:, :hop]
        mask[pl.ds(start, rows), :] = block[:, hop:]
    xs[segs * rows :, :] = jnp.zeros((rows, hop), F32)
    count = segs * rows

    spectra(xs, count, rows, small, step_table, lhs, z)
    for at in range(0, count, 8):

        def put(p, x, y):
            out[p, at : at + 8, :LANES] = x
            out[p, at : at + 8, LANES:] = y

        whiten(z, count, at, small, put)


def stack_kernel(segs, hops, spectrum, mask, *refs):
    count = max(hops, 1)
    pay = refs[:count]
    small, step_table, lag, out = refs[count : count + 4]
    xs, lhs, z, near, prod = refs[count + 4 :]
    hop = pay[0].shape[1] - LANES
    rows = mask.shape[0] // segs
    group = lax.axis_index("recv")
    me = lax.axis_index("tm")
    sources = sum(p.shape[0] for p in pay) // segs
    if hops:
        per_part = sources // 2
        for hop_no, part in enumerate(pay):
            side, sender = holder(hop_no, group // 2, group % 2, me, segs)
            for half in range(2):
                for k in range(2):
                    for i in range(per_part):
                        row = (2 * half + k) * per_part + i
                        at = (sender ^ k) * sources + (side ^ half) * per_part + i
                        xs[pl.ds(at, 1), :] = part[row : row + 1, :]
    else:
        xs[: segs * sources, :] = pay[0][...]
    xs[segs * sources :, :] = jnp.zeros((sources, hop + LANES), F32)
    count = segs * sources
    spectra(xs, count, sources, small, step_table, lhs, z)
    for first in range(0, count, 8):

        def put(p, x, y):
            near[p, first : first + 8, :LANES] = x
            near[p, first : first + 8, LANES:] = y

        whiten(z, count, first, small, put)
    size = count * rows
    for p in range(PAIRS):
        for k in range(segs):
            rx, ry = (spectrum[p, k * rows : (k + 1) * rows, c * LANES : (c + 1) * LANES] for c in range(2))
            for s in range(sources):
                i = k * sources + s
                sx, sy = (near[p, i : i + 1, c * LANES : (c + 1) * LANES] for c in range(2))
                for c, cross in enumerate((sx * rx + sy * ry, sx * ry - sy * rx)):
                    cols = slice((2 * p + c) * LANES, (2 * p + c + 1) * LANES)
                    high, low = split(cross)
                    prod[i * rows : (i + 1) * rows, cols] = high
                    prod[size + i * rows : size + (i + 1) * rows, cols] = low
    both = dot(prod[...], lag[0])
    total = both[:size] + both[size:] + dot(prod[:size, :], lag[1])
    scale = lax.rsqrt(jnp.mean(total * total, axis=1, keepdims=True) + 1e-6)
    for s in range(sources):
        stack = None
        for k in range(segs):
            i = k * sources + s
            weight = mask[k * rows : (k + 1) * rows, 0:1] * xs[i : i + 1, hop : hop + 1]
            term = total[i * rows : (i + 1) * rows, :] * (weight * scale[i * rows : (i + 1) * rows, :])
            stack = term if stack is None else stack + term
        out[s] = stack


def chosen(values, index):
    if isinstance(index, int):
        return values[index]
    return sum(jnp.where(index == i, value, 0) for i, value in enumerate(values))


def holder(hop, place, side, me, segs):
    packed = chosen(ROUTES[hop], me) >> (3 * (2 * place + side))
    return packed & 1, 2 * ((packed >> 2) & 1) + ((packed >> 1) & 1)


def vmem(count):
    return [pl.BlockSpec(memory_space=pltpu.VMEM)] * count


PARAMS = dict(compiler_params=pltpu.CompilerParams(vmem_limit_bytes=32 * 1024 * 1024))


def other(value, segs, k):
    return lax.ppermute(value, "tm", [(i, i ^ k) for i in range(segs)])


def local(record, source_channels, valid_mask):
    rows, hop = record.shape
    segs = lax.axis_size("tm")
    groups = lax.axis_size("recv")
    sources = source_channels.shape[0]
    mine = sources // segs
    width = hop + LANES
    constant, step_constant = [pltpu.with_memory_space_constraint(c, pltpu.HBM) for c in tables(2 * hop)]
    hbm = pl.BlockSpec(memory_space=pltpu.HBM)
    fast = segs == 4 and groups == 2 * segs and sources % groups == 0
    per_group = sources // groups if fast else 0
    payload, small, step_table, *piece = pl.pallas_call(
        functools.partial(join_kernel, per_group),
        out_shape=(
            jax.ShapeDtypeStruct((rows, width), F32),
            jax.ShapeDtypeStruct(constant.shape, F32),
            jax.ShapeDtypeStruct(step_constant.shape, BF),
            *[jax.ShapeDtypeStruct((per_group, width), F32)] * fast,
        ),
        in_specs=[hbm] * 5,
        out_specs=tuple(vmem(3 + fast)),
        scratch_shapes=[
            pltpu.VMEM((1, rows), jnp.int32),
            pltpu.SMEM((sources,), jnp.int32),
            pltpu.SemaphoreType.DMA((5,)),
        ],
        name="join",
        **PARAMS,
    )(*[pltpu.with_memory_space_constraint(a, pltpu.HBM) for a in (record, valid_mask.reshape(1, rows), source_channels)], constant, step_constant)
    lag = pl.pallas_call(
        lag_kernel,
        out_shape=jax.ShapeDtypeStruct((2, RADIX * LANES, LAGS), BF),
        in_specs=vmem(1),
        out_specs=pl.BlockSpec(memory_space=pltpu.VMEM),
        name="waves",
        **PARAMS,
    )(small)
    blocks = [payload] + [other(payload, segs, k) for k in range(1, segs)]
    if fast:
        hops = segs // 2
        neighbour, lag = lax.optimization_barrier((other(piece[0], segs, 1), lag))
        pair = jnp.concatenate([piece[0], neighbour], axis=0)
        beside = lax.ppermute(pair, "recv", [(r, r ^ 1) for r in range(groups)])
        picked = jnp.concatenate([pair, beside], axis=0)
        pay = []
        for hop_no in range(hops):
            route = []
            for r in range(groups):
                for t in range(segs):
                    side, sender = holder(hop_no, r // 2, r % 2, t, segs)
                    route.append(((2 * t + side) * segs + sender, r * segs + t))
            pay.append(lax.ppermute(picked, ("recv", "tm"), route))
    else:
        hops = 0
        row = source_channels - lax.axis_index("recv") * rows
        here = (row >= 0) & (row < rows)
        mine_now = jnp.where(here[:, None], payload[jnp.clip(row, 0, rows - 1)], 0.0)
        whole = lax.psum(mine_now, "recv").reshape(segs, mine, width)
        whole = lax.all_to_all(whole, "tm", 0, 0)
        pay = [whole.reshape(segs * mine, width)]

    count = segs * rows
    spectrum, weights = pl.pallas_call(
        functools.partial(receiver_kernel, segs),
        out_shape=(
            jax.ShapeDtypeStruct((PAIRS, count, 2 * LANES), F32),
            jax.ShapeDtypeStruct((count, LANES), F32),
        ),
        in_specs=vmem(segs + 2),
        out_specs=tuple(vmem(2)),
        scratch_shapes=[
            pltpu.VMEM((count + rows, hop), F32),
            pltpu.VMEM((2 * RADIX * count, 2 * LANES), BF),
            pltpu.VMEM((RADIX * count, LANES), F32),
        ],
        name="receivers",
        **PARAMS,
    )(*blocks, small, step_table)

    src_count = segs * mine
    return pl.pallas_call(
        functools.partial(stack_kernel, segs, hops),
        out_shape=jax.ShapeDtypeStruct((mine, rows, LAGS), F32),
        in_specs=vmem(5 + len(pay)),
        out_specs=pl.BlockSpec(memory_space=pltpu.VMEM),
        scratch_shapes=[
            pltpu.VMEM((src_count + mine, width), F32),
            pltpu.VMEM((2 * RADIX * src_count, 2 * LANES), BF),
            pltpu.VMEM((RADIX * src_count, LANES), F32),
            pltpu.VMEM((PAIRS, src_count, 2 * LANES), F32),
            pltpu.VMEM((2 * src_count * rows, RADIX * LANES), BF),
        ],
        name="stacks",
        **PARAMS,
    )(spectrum, weights, *pay, small, step_table, lag)


def solution(mesh):
    placed = (P("recv", "tm"), P(), P("recv", "tm"))
    return jax.shard_map(
        local, mesh=mesh, in_specs=placed, out_specs=P("tm", "recv", None), check_vma=False
    )
```

```python
import functools

import jax
import jax.numpy as jnp
import ml_dtypes
import numpy as np
from jax import lax
from jax.experimental import pallas as pl
from jax.experimental.pallas import tpu as pltpu
from jax.sharding import PartitionSpec as P

LANES = 128
LAGS = 256
SMOOTH = 64
RADIX = 16
PAIRS = RADIX // 2
ROUTES = ((16288538, 6472634, 2894654, 14524972), (2279102, 11640342, 15946392, 7032648))
BF = jnp.bfloat16
F32 = jnp.float32


def order():
    return np.arange(PAIRS)[:, None] + PAIRS * np.arange(2)


def halves(table):
    high = table.astype(ml_dtypes.bfloat16)
    return np.stack([high, (table - high.astype(np.float64)).astype(ml_dtypes.bfloat16)])


@functools.cache
def tables(seglen):
    bins = seglen // 2
    keep = bins // RADIX
    samples = np.arange(seglen)
    taper = (0.5 - 0.5 * np.cos(2 * np.pi * samples / seglen)).reshape(RADIX, LANES)
    n2 = np.arange(LANES)[:, None]
    angle = 2 * np.pi * ((n2 * np.arange(keep)[None, :]) % LANES) / LANES
    cos, sin = np.cos(angle), np.sin(angle)
    step = np.concatenate(list(halves(np.block([[cos, -sin], [-sin, -cos]]))), axis=1)
    angle = 2 * np.pi * (np.arange(RADIX)[:, None] * n2.T) / seglen
    f = order()[:, :, None] + RADIX * np.arange(keep)
    counts = np.minimum(f + SMOOTH, bins - 1) - np.maximum(f - SMOOTH, 0) + 1
    inverse_counts = (1.0 / counts).reshape(PAIRS, LANES)
    f2 = np.arange(keep)[:, None]
    angle_low = 2 * np.pi * ((f2 * np.arange(LANES)) % LANES) / LANES
    lags = np.arange(LAGS) - LAGS // 2
    angle_high = 2 * np.pi * np.arange(RADIX)[:, None] * lags / seglen
    factor = 2.0 / seglen
    small = [
        taper,
        np.cos(angle),
        np.sin(angle),
        inverse_counts,
        np.cos(angle_low),
        np.sin(angle_low),
        factor * np.cos(angle_high).reshape(-1, LANES),
        factor * np.sin(angle_high).reshape(-1, LANES),
    ]
    return np.concatenate(small).astype(np.float32), step


def radix_step(x):
    r = float(np.sqrt(0.5))
    c1 = float(np.cos(np.pi / 8))
    c3 = float(np.cos(3 * np.pi / 8))
    c = [None] + [x[n] + x[16 - n] for n in range(1, 8)]
    s = [None] + [x[n] - x[16 - n] for n in range(1, 8)]
    e = [x[0] + x[8]] + [c[n] + c[8 - n] for n in range(1, 4)] + [c[4]]
    o = [x[0] - x[8]] + [c[n] - c[8 - n] for n in range(1, 4)]
    g = [None] + [s[n] - s[8 - n] for n in range(1, 4)]
    h = [None] + [s[n] + s[8 - n] for n in range(1, 4)] + [s[4]]
    e04 = e[0] + e[4]
    e04m = e[0] - e[4]
    e13 = e[1] + e[3]
    e13m = r * (e[1] - e[3])
    e042 = e04 + e[2]
    g13 = r * (g[1] + g[3])
    o2 = r * o[2]
    h2 = r * h[2]
    re = {
        0: e042 + e13,
        8: e042 - e13,
        4: e04 - e[2],
        2: e04m + e13m,
        6: e04m - e13m,
        1: (o[0] + o2) + (c1 * o[1] + c3 * o[3]),
        7: (o[0] + o2) - (c1 * o[1] + c3 * o[3]),
        3: (o[0] - o2) + (c3 * o[1] - c1 * o[3]),
        5: (o[0] - o2) - (c3 * o[1] - c1 * o[3]),
    }
    im = {
        2: g13 + g[2],
        4: g[1] - g[3],
        6: g13 - g[2],
        1: (h2 + h[4]) + (c3 * h[1] + c1 * h[3]),
        7: (c3 * h[1] + c1 * h[3]) - (h2 + h[4]),
        3: (h2 - h[4]) + (c1 * h[1] - c3 * h[3]),
        5: (c1 * h[1] - c3 * h[3]) - (h2 - h[4]),
    }
    return re, im


def split(value):
    high = value.astype(BF)
    return high, (value - high.astype(F32)).astype(BF)


def dot(a, b):
    return jnp.dot(a, b, preferred_element_type=F32)


def spectra(xs, count, shift, small, step_table, lhs, z):
    seglen = RADIX * LANES
    step = 16
    every = RADIX * count

    def group(first):
        x = [xs[first : first + step, n * LANES : (n + 1) * LANES] for n in range(PAIRS)]
        x += [xs[first + shift : first + shift + step, n * LANES : (n + 1) * LANES] for n in range(PAIRS)]
        total = x[0]
        for part in x[1:]:
            total = total + part
        mean = jnp.sum(total, axis=1, keepdims=True) * (1.0 / seglen)
        x = [(x[n] - mean) * small[n : n + 1, :] for n in range(RADIX)]
        re, im = radix_step(x)
        for p in range(PAIRS):
            for half in range(2):
                f1 = p + PAIRS * half
                cos, sin = small[RADIX + f1 : RADIX + f1 + 1, :], small[2 * RADIX + f1 : 2 * RADIX + f1 + 1, :]
                if f1 == 0:
                    parts = (re[0], jnp.zeros_like(re[0]))
                elif f1 == PAIRS:
                    parts = (re[f1] * cos, re[f1] * sin)
                elif f1 < PAIRS:
                    parts = (re[f1] * cos - im[f1] * sin, re[f1] * sin + im[f1] * cos)
                else:
                    a, b = re[RADIX - f1], im[RADIX - f1]
                    parts = (a * cos + b * sin, a * sin - b * cos)
                for i, part in enumerate(parts):
                    high, low = split(part)
                    cols = slice(i * LANES, (i + 1) * LANES)
                    at = f1 * count + first
                    lhs[at : at + step, cols] = high
                    lhs[every + at : every + at + step, cols] = low

    for first in range(0, count, step):
        group(first)
    both = dot(lhs[...], step_table[...])
    both = both[:, :LANES] + both[:, LANES:]
    z[...] = both[:every] + both[every:]


def whiten(z, count, first, height, small, put):
    keep = LANES // 2
    lane = lax.broadcasted_iota(jnp.int32, (height, LANES), 1)
    place = lane % keep
    upper = lane >= keep
    blocks = []
    for p in range(PAIRS):
        a = z[p * count + first : p * count + first + height, :]
        b = z[(p + PAIRS) * count + first : (p + PAIRS) * count + first + height, :]
        blocks.append((jnp.where(upper, pltpu.roll(b, keep, 1), a), jnp.where(upper, b, pltpu.roll(a, keep, 1))))
    power = [x * x + y * y for x, y in blocks]
    upto = [power[0]]
    for p in range(1, PAIRS):
        upto.append(upto[-1] + power[p])
    since = [power[PAIRS - 1]]
    for p in range(PAIRS - 2, -1, -1):
        since.append(since[-1] + power[p])
    since = since[::-1]
    half = upto[-1]
    reach = SMOOTH // RADIX

    def moved(value, by):
        inside = (place < keep - by) if by > 0 else (place >= -by)
        return jnp.where(inside, pltpu.roll(value, -by % LANES, 1), 0.0)

    def across(by):
        if by == 0:
            return pltpu.roll(half, keep, 1)
        inside = (place < keep - by) if by > 0 else (place >= -by)
        return jnp.where(inside, pltpu.roll(half, (keep - by) % LANES, 1), 0.0)

    inner = half + across(0)
    for by in range(1, reach):
        inner = inner + ((moved(half, by) + moved(half, -by)) + (across(by) + across(-by)))
    inner = inner + (jnp.where(upper, across(reach), 0.0) + jnp.where(upper, 0.0, across(-reach)))
    for p, (x, y) in enumerate(blocks):
        window = inner + (moved(since[p], -reach) + moved(upto[p], reach))
        scale = lax.rsqrt(window * small[3 * RADIX + p : 3 * RADIX + p + 1, :] + 1e-6)
        put(p, x * scale, y * scale)


def join_kernel(per_group, record, valid, src, constant, step_constant, out, small, step_table, *refs):
    *picked, row, channels, sems = refs
    rows, hop = record.shape
    copies = [
        pltpu.make_async_copy(src, channels, sems.at[0]),
        pltpu.make_async_copy(valid, row, sems.at[1]),
        pltpu.make_async_copy(record, out.at[:, pl.ds(0, hop)], sems.at[2]),
        pltpu.make_async_copy(constant, small, sems.at[3]),
        pltpu.make_async_copy(step_constant, step_table, sems.at[4]),
    ]
    for copy in copies:
        copy.start()
    copies[1].wait()
    square = (rows, rows)
    here = lax.broadcasted_iota(jnp.int32, square, 0) == lax.broadcasted_iota(jnp.int32, square, 1)
    column = jnp.sum(jnp.where(here, row[...].astype(F32), 0.0), axis=1, keepdims=True)
    out[:, hop:] = jnp.broadcast_to(column, (rows, LANES))
    copies[0].wait()
    copies[2].wait()
    first = lax.axis_index("recv")
    for i in range(per_group):
        place = channels[first * per_group + i] - first * rows
        picked[0][i : i + 1, :] = out[pl.ds(place, 1), :]
    copies[3].wait()
    copies[4].wait()


def lag_kernel(small, lag):
    keep = LANES // 2
    step = 16
    low = 3 * RADIX + PAIRS
    high = low + 2 * keep
    wide = LAGS // LANES
    first = lax.broadcasted_iota(jnp.int32, (step, LANES), 0) == 0
    for f1 in range(RADIX):
        for h in range(wide):
            at = high + f1 * wide + h
            cos_high = small[at : at + 1, :]
            sin_high = small[at + RADIX * wide : at + RADIX * wide + 1, :]
            for f2 in range(0, keep, step):
                cos_low = small[low + f2 : low + f2 + step, :]
                sin_low = small[low + keep + f2 : low + keep + f2 + step, :]
                cos = cos_high * cos_low - sin_high * sin_low
                sin = sin_high * cos_low + cos_high * sin_low
                if f1 == 0 and f2 == 0:
                    cos = jnp.where(first, 0.5 * cos, cos)
                    sin = jnp.where(first, 0.5 * sin, sin)
                for c, value in enumerate((cos, -sin)):
                    row = (2 * (f1 % PAIRS) + c) * LANES + (f1 // PAIRS) * keep + f2
                    for i, part in enumerate(split(value)):
                        lag[i, row : row + step, h * LANES : (h + 1) * LANES] = part


def receiver_kernel(segs, *refs):
    blocks = refs[:segs]
    small, step_table, out, mask, xs, lhs, z = refs[segs:]
    rows, width = blocks[0].shape
    hop = width - LANES
    me = lax.axis_index("tm")
    for k, block in enumerate(blocks):
        start = pl.multiple_of((me ^ k) * rows, rows)
        xs[pl.ds(start, rows), :] = block[:, :hop]
        mask[pl.ds(start, rows), :] = block[:, hop:]
    xs[segs * rows :, :] = jnp.zeros((rows, hop), F32)
    count = segs * rows

    spectra(xs, count, rows, small, step_table, lhs, z)
    for at in range(0, count, 8):

        def put(p, x, y):
            out[p, at : at + 8, :LANES] = x
            out[p, at : at + 8, LANES:] = y

        whiten(z, count, at, 8, small, put)


def stack_kernel(segs, hops, spectrum, mask, *refs):
    count = max(hops, 1)
    pay = refs[:count]
    small, step_table, lag, out = refs[count : count + 4]
    xs, lhs, z, near, *prod = refs[count + 4 :]
    hop = pay[0].shape[1] - LANES
    rows = mask.shape[0] // segs
    group = lax.axis_index("recv")
    me = lax.axis_index("tm")
    sources = sum(p.shape[0] for p in pay) // segs
    if hops:
        per_part = sources // 2
        for hop_no, part in enumerate(pay):
            side, sender = holder(hop_no, group // 2, group % 2, me, segs)
            for half in range(2):
                for k in range(2):
                    for i in range(per_part):
                        row = (2 * half + k) * per_part + i
                        at = (sender ^ k) * sources + (side ^ half) * per_part + i
                        xs[pl.ds(at, 1), :] = part[row : row + 1, :]
    else:
        xs[: segs * sources, :] = pay[0][...]
    xs[segs * sources :, :] = jnp.zeros((sources, hop + LANES), F32)
    count = segs * sources
    spectra(xs, count, sources, small, step_table, lhs, z)

    def put(p, x, y):
        near[p, :, :LANES] = x
        near[p, :, LANES:] = y

    whiten(z, count, 0, count, small, put)
    size = count * rows
    total = None
    for p in range(PAIRS):
        for k in range(segs):
            rx, ry = (spectrum[p, k * rows : (k + 1) * rows, c * LANES : (c + 1) * LANES] for c in range(2))
            for s in range(sources):
                i = k * sources + s
                sx, sy = (near[p, i : i + 1, c * LANES : (c + 1) * LANES] for c in range(2))
                for c, cross in enumerate((sx * rx + sy * ry, sx * ry - sy * rx)):
                    cols = slice(c * LANES, (c + 1) * LANES)
                    high, low = split(cross)
                    prod[p][i * rows : (i + 1) * rows, cols] = high
                    prod[p][size + i * rows : size + (i + 1) * rows, cols] = low
        depth = slice(2 * p * LANES, (2 * p + 2) * LANES)
        both = dot(prod[p][...], lag[0, depth, :])
        part = both[:size] + both[size:] + dot(prod[p][:size, :], lag[1, depth, :])
        total = part if total is None else total + part
    scale = lax.rsqrt(jnp.mean(total * total, axis=1, keepdims=True) + 1e-6)
    for s in range(sources):
        stack = None
        for k in range(segs):
            i = k * sources + s
            weight = mask[k * rows : (k + 1) * rows, 0:1] * xs[i : i + 1, hop : hop + 1]
            term = total[i * rows : (i + 1) * rows, :] * (weight * scale[i * rows : (i + 1) * rows, :])
            stack = term if stack is None else stack + term
        out[s] = stack


def chosen(values, index):
    if isinstance(index, int):
        return values[index]
    return sum(jnp.where(index == i, value, 0) for i, value in enumerate(values))


def holder(hop, place, side, me, segs):
    packed = chosen(ROUTES[hop], me) >> (3 * (2 * place + side))
    return packed & 1, 2 * ((packed >> 2) & 1) + ((packed >> 1) & 1)


def vmem(count):
    return [pl.BlockSpec(memory_space=pltpu.VMEM)] * count


PARAMS = dict(compiler_params=pltpu.CompilerParams(vmem_limit_bytes=32 * 1024 * 1024))


def other(value, segs, k):
    return lax.ppermute(value, "tm", [(i, i ^ k) for i in range(segs)])


def local(record, source_channels, valid_mask):
    rows, hop = record.shape
    segs = lax.axis_size("tm")
    groups = lax.axis_size("recv")
    sources = source_channels.shape[0]
    mine = sources // segs
    width = hop + LANES
    constant, step_constant = [pltpu.with_memory_space_constraint(c, pltpu.HBM) for c in tables(2 * hop)]
    hbm = pl.BlockSpec(memory_space=pltpu.HBM)
    fast = segs == 4 and groups == 2 * segs and sources % groups == 0
    per_group = sources // groups if fast else 0
    payload, small, step_table, *piece = pl.pallas_call(
        functools.partial(join_kernel, per_group),
        out_shape=(
            jax.ShapeDtypeStruct((rows, width), F32),
            jax.ShapeDtypeStruct(constant.shape, F32),
            jax.ShapeDtypeStruct(step_constant.shape, BF),
            *[jax.ShapeDtypeStruct((per_group, width), F32)] * fast,
        ),
        in_specs=[hbm] * 5,
        out_specs=tuple(vmem(3 + fast)),
        scratch_shapes=[
            pltpu.VMEM((1, rows), jnp.int32),
            pltpu.SMEM((sources,), jnp.int32),
            pltpu.SemaphoreType.DMA((5,)),
        ],
        name="join",
        **PARAMS,
    )(*[pltpu.with_memory_space_constraint(a, pltpu.HBM) for a in (record, valid_mask.reshape(1, rows), source_channels)], constant, step_constant)
    lag = pl.pallas_call(
        lag_kernel,
        out_shape=jax.ShapeDtypeStruct((2, RADIX * LANES, LAGS), BF),
        in_specs=vmem(1),
        out_specs=pl.BlockSpec(memory_space=pltpu.VMEM),
        name="waves",
        **PARAMS,
    )(small)
    blocks = [payload] + [other(payload, segs, k) for k in range(1, segs)]
    if fast:
        hops = segs // 2
        pieces = [piece[0]]
        for side, bit in ((0, 1), (1, 0), (1, 1)):
            route = [(r * segs + t, (r ^ side) * segs + (t ^ bit)) for r in range(groups) for t in range(segs)]
            pieces.append(lax.ppermute(piece[0], ("recv", "tm"), route))
        pieces, lag = lax.optimization_barrier((pieces, lag))
        picked = jnp.concatenate(pieces, axis=0)
        pay = []
        for hop_no in range(hops):
            route = []
            for r in range(groups):
                for t in range(segs):
                    side, sender = holder(hop_no, r // 2, r % 2, t, segs)
                    route.append(((2 * t + side) * segs + sender, r * segs + t))
            pay.append(lax.ppermute(picked, ("recv", "tm"), route))
    else:
        hops = 0
        row = source_channels - lax.axis_index("recv") * rows
        here = (row >= 0) & (row < rows)
        mine_now = jnp.where(here[:, None], payload[jnp.clip(row, 0, rows - 1)], 0.0)
        whole = lax.psum(mine_now, "recv").reshape(segs, mine, width)
        whole = lax.all_to_all(whole, "tm", 0, 0)
        pay = [whole.reshape(segs * mine, width)]

    count = segs * rows
    spectrum, weights = pl.pallas_call(
        functools.partial(receiver_kernel, segs),
        out_shape=(
            jax.ShapeDtypeStruct((PAIRS, count, 2 * LANES), F32),
            jax.ShapeDtypeStruct((count, LANES), F32),
        ),
        in_specs=vmem(segs + 2),
        out_specs=tuple(vmem(2)),
        scratch_shapes=[
            pltpu.VMEM((count + rows, hop), F32),
            pltpu.VMEM((2 * RADIX * count, 2 * LANES), BF),
            pltpu.VMEM((RADIX * count, LANES), F32),
        ],
        name="receivers",
        **PARAMS,
    )(*blocks, small, step_table)

    src_count = segs * mine
    return pl.pallas_call(
        functools.partial(stack_kernel, segs, hops),
        out_shape=jax.ShapeDtypeStruct((mine, rows, LAGS), F32),
        in_specs=vmem(5 + len(pay)),
        out_specs=pl.BlockSpec(memory_space=pltpu.VMEM),
        scratch_shapes=[
            pltpu.VMEM((src_count + mine, width), F32),
            pltpu.VMEM((2 * RADIX * src_count, 2 * LANES), BF),
            pltpu.VMEM((RADIX * src_count, LANES), F32),
            pltpu.VMEM((PAIRS, src_count, 2 * LANES), F32),
            *[pltpu.VMEM((2 * src_count * rows, 2 * LANES), BF)] * PAIRS,
        ],
        name="stacks",
        **PARAMS,
    )(spectrum, weights, *pay, small, step_table, lag)


def solution(mesh):
    placed = (P("recv", "tm"), P(), P("recv", "tm"))
    return jax.shard_map(
        local, mesh=mesh, in_specs=placed, out_specs=P("tm", "recv", None), check_vma=False
    )
```

```python
import functools

import jax
import jax.numpy as jnp
import ml_dtypes
import numpy as np
from jax import lax
from jax.experimental import pallas as pl
from jax.experimental.pallas import tpu as pltpu
from jax.sharding import PartitionSpec as P

LANES = 128
LAGS = 256
SMOOTH = 64
RADIX = 16
PAIRS = RADIX // 2
ROUTES = ((16288538, 2345882, 350014, 8161454), (2279102, 11637822, 11779208, 11256728))
BF = jnp.bfloat16
F32 = jnp.float32


def order():
    return np.arange(PAIRS)[:, None] + PAIRS * np.arange(2)


def halves(table):
    high = table.astype(ml_dtypes.bfloat16)
    return np.stack([high, (table - high.astype(np.float64)).astype(ml_dtypes.bfloat16)])


@functools.cache
def tables(seglen):
    bins = seglen // 2
    keep = bins // RADIX
    samples = np.arange(seglen)
    taper = (0.5 - 0.5 * np.cos(2 * np.pi * samples / seglen)).reshape(RADIX, LANES)
    n2 = np.arange(LANES)[:, None]
    angle = 2 * np.pi * ((n2 * np.arange(keep)[None, :]) % LANES) / LANES
    cos, sin = np.cos(angle), np.sin(angle)
    step = np.concatenate(list(halves(np.block([[cos, -sin], [-sin, -cos]]))), axis=1)
    angle = 2 * np.pi * (np.arange(RADIX)[:, None] * n2.T) / seglen
    f = order()[:, :, None] + RADIX * np.arange(keep)
    counts = np.minimum(f + SMOOTH, bins - 1) - np.maximum(f - SMOOTH, 0) + 1
    inverse_counts = (1.0 / counts).reshape(PAIRS, LANES)
    f2 = np.arange(keep)[:, None]
    angle_low = 2 * np.pi * ((f2 * np.arange(LANES)) % LANES) / LANES
    lags = np.arange(LAGS) - LAGS // 2
    angle_high = 2 * np.pi * np.arange(RADIX)[:, None] * lags / seglen
    factor = 2.0 / seglen
    small = [taper, np.cos(angle), np.sin(angle), inverse_counts]
    waves = [
        np.cos(angle_low),
        np.sin(angle_low),
        factor * np.cos(angle_high).reshape(-1, LANES),
        factor * np.sin(angle_high).reshape(-1, LANES),
    ]
    return np.concatenate(small).astype(np.float32), step, np.concatenate(waves).astype(np.float32)


def radix_step(x):
    r = float(np.sqrt(0.5))
    c1 = float(np.cos(np.pi / 8))
    c3 = float(np.cos(3 * np.pi / 8))
    c = [None] + [x[n] + x[16 - n] for n in range(1, 8)]
    s = [None] + [x[n] - x[16 - n] for n in range(1, 8)]
    e = [x[0] + x[8]] + [c[n] + c[8 - n] for n in range(1, 4)] + [c[4]]
    o = [x[0] - x[8]] + [c[n] - c[8 - n] for n in range(1, 4)]
    g = [None] + [s[n] - s[8 - n] for n in range(1, 4)]
    h = [None] + [s[n] + s[8 - n] for n in range(1, 4)] + [s[4]]
    e04 = e[0] + e[4]
    e04m = e[0] - e[4]
    e13 = e[1] + e[3]
    e13m = r * (e[1] - e[3])
    e042 = e04 + e[2]
    g13 = r * (g[1] + g[3])
    o2 = r * o[2]
    h2 = r * h[2]
    re = {
        0: e042 + e13,
        8: e042 - e13,
        4: e04 - e[2],
        2: e04m + e13m,
        6: e04m - e13m,
        1: (o[0] + o2) + (c1 * o[1] + c3 * o[3]),
        7: (o[0] + o2) - (c1 * o[1] + c3 * o[3]),
        3: (o[0] - o2) + (c3 * o[1] - c1 * o[3]),
        5: (o[0] - o2) - (c3 * o[1] - c1 * o[3]),
    }
    im = {
        2: g13 + g[2],
        4: g[1] - g[3],
        6: g13 - g[2],
        1: (h2 + h[4]) + (c3 * h[1] + c1 * h[3]),
        7: (c3 * h[1] + c1 * h[3]) - (h2 + h[4]),
        3: (h2 - h[4]) + (c1 * h[1] - c3 * h[3]),
        5: (c1 * h[1] - c3 * h[3]) - (h2 - h[4]),
    }
    return re, im


def split(value):
    high = value.astype(BF)
    return high, (value - high.astype(F32)).astype(BF)


def dot(a, b):
    return jnp.dot(a, b, preferred_element_type=F32)


def spectra(xs, count, shift, small, step_table, lhs, z):
    seglen = RADIX * LANES
    step = 16
    every = RADIX * count

    def group(first):
        x = [xs[first : first + step, n * LANES : (n + 1) * LANES] for n in range(PAIRS)]
        x += [xs[first + shift : first + shift + step, n * LANES : (n + 1) * LANES] for n in range(PAIRS)]
        total = x[0]
        for part in x[1:]:
            total = total + part
        mean = jnp.sum(total, axis=1, keepdims=True) * (1.0 / seglen)
        x = [(x[n] - mean) * small[n : n + 1, :] for n in range(RADIX)]
        re, im = radix_step(x)
        for p in range(PAIRS):
            for half in range(2):
                f1 = p + PAIRS * half
                cos, sin = small[RADIX + f1 : RADIX + f1 + 1, :], small[2 * RADIX + f1 : 2 * RADIX + f1 + 1, :]
                if f1 == 0:
                    parts = (re[0], jnp.zeros_like(re[0]))
                elif f1 == PAIRS:
                    parts = (re[f1] * cos, re[f1] * sin)
                elif f1 < PAIRS:
                    parts = (re[f1] * cos - im[f1] * sin, re[f1] * sin + im[f1] * cos)
                else:
                    a, b = re[RADIX - f1], im[RADIX - f1]
                    parts = (a * cos + b * sin, a * sin - b * cos)
                for i, part in enumerate(parts):
                    high, low = split(part)
                    cols = slice(i * LANES, (i + 1) * LANES)
                    at = f1 * count + first
                    lhs[at : at + step, cols] = high
                    lhs[every + at : every + at + step, cols] = low

    for first in range(0, count, step):
        group(first)
    both = dot(lhs[...], step_table[...])
    both = both[:, :LANES] + both[:, LANES:]
    z[...] = both[:every] + both[every:]


def whiten(z, count, first, height, small, put):
    keep = LANES // 2
    lane = lax.broadcasted_iota(jnp.int32, (height, LANES), 1)
    place = lane % keep
    upper = lane >= keep
    blocks = []
    for p in range(PAIRS):
        a = z[p * count + first : p * count + first + height, :]
        b = z[(p + PAIRS) * count + first : (p + PAIRS) * count + first + height, :]
        blocks.append((jnp.where(upper, pltpu.roll(b, keep, 1), a), jnp.where(upper, b, pltpu.roll(a, keep, 1))))
    power = [x * x + y * y for x, y in blocks]
    upto = [power[0]]
    for p in range(1, PAIRS):
        upto.append(upto[-1] + power[p])
    since = [power[PAIRS - 1]]
    for p in range(PAIRS - 2, -1, -1):
        since.append(since[-1] + power[p])
    since = since[::-1]
    half = upto[-1]
    reach = SMOOTH // RADIX

    def moved(value, by):
        inside = (place < keep - by) if by > 0 else (place >= -by)
        return jnp.where(inside, pltpu.roll(value, -by % LANES, 1), 0.0)

    def across(by):
        if by == 0:
            return pltpu.roll(half, keep, 1)
        inside = (place < keep - by) if by > 0 else (place >= -by)
        return jnp.where(inside, pltpu.roll(half, (keep - by) % LANES, 1), 0.0)

    inner = half + across(0)
    for by in range(1, reach):
        inner = inner + ((moved(half, by) + moved(half, -by)) + (across(by) + across(-by)))
    inner = inner + (jnp.where(upper, across(reach), 0.0) + jnp.where(upper, 0.0, across(-reach)))
    for p, (x, y) in enumerate(blocks):
        window = inner + (moved(since[p], -reach) + moved(upto[p], reach))
        scale = lax.rsqrt(window * small[3 * RADIX + p : 3 * RADIX + p + 1, :] + 1e-6)
        put(p, x * scale, y * scale)


def join_kernel(per_group, record, valid, src, constant, out, waves, *refs):
    *picked, row, channels, sems = refs
    rows, hop = record.shape
    copies = [
        pltpu.make_async_copy(src, channels, sems.at[0]),
        pltpu.make_async_copy(valid, row, sems.at[1]),
        pltpu.make_async_copy(record, out.at[:, pl.ds(0, hop)], sems.at[2]),
        pltpu.make_async_copy(constant, waves, sems.at[3]),
    ]
    for copy in copies:
        copy.start()
    copies[1].wait()
    square = (rows, rows)
    here = lax.broadcasted_iota(jnp.int32, square, 0) == lax.broadcasted_iota(jnp.int32, square, 1)
    column = jnp.sum(jnp.where(here, row[...].astype(F32), 0.0), axis=1, keepdims=True)
    out[:, hop:] = jnp.broadcast_to(column, (rows, LANES))
    copies[0].wait()
    copies[2].wait()
    first = lax.axis_index("recv")
    for i in range(per_group):
        place = channels[first * per_group + i] - first * rows
        picked[0][i : i + 1, :] = out[pl.ds(place, 1), :]
    copies[3].wait()


def lag_kernel(waves, lag):
    keep = LANES // 2
    step = 16
    low = 0
    high = 2 * keep
    wide = LAGS // LANES
    first = lax.broadcasted_iota(jnp.int32, (step, LANES), 0) == 0
    for f1 in range(RADIX):
        for h in range(wide):
            at = high + f1 * wide + h
            cos_high = waves[at : at + 1, :]
            sin_high = waves[at + RADIX * wide : at + RADIX * wide + 1, :]
            for f2 in range(0, keep, step):
                cos_low = waves[low + f2 : low + f2 + step, :]
                sin_low = waves[low + keep + f2 : low + keep + f2 + step, :]
                cos = cos_high * cos_low - sin_high * sin_low
                sin = sin_high * cos_low + cos_high * sin_low
                if f1 == 0 and f2 == 0:
                    cos = jnp.where(first, 0.5 * cos, cos)
                    sin = jnp.where(first, 0.5 * sin, sin)
                for c, value in enumerate((cos, -sin)):
                    row = (2 * (f1 % PAIRS) + c) * LANES + (f1 // PAIRS) * keep + f2
                    for i, part in enumerate(split(value)):
                        lag[i, row : row + step, h * LANES : (h + 1) * LANES] = part


def receiver_kernel(segs, *refs):
    blocks = refs[:segs]
    small, step_table, out, mask, xs, lhs, z = refs[segs:]
    rows, width = blocks[0].shape
    hop = width - LANES
    me = lax.axis_index("tm")
    for k, block in enumerate(blocks):
        start = pl.multiple_of((me ^ k) * rows, rows)
        xs[pl.ds(start, rows), :] = block[:, :hop]
        mask[pl.ds(start, rows), :] = block[:, hop:]
    xs[segs * rows :, :] = jnp.zeros((rows, hop), F32)
    count = segs * rows

    spectra(xs, count, rows, small, step_table, lhs, z)
    for at in range(0, count, 16):

        def put(p, x, y):
            out[p, at : at + 16, :LANES] = x
            out[p, at : at + 16, LANES:] = y

        whiten(z, count, at, 16, small, put)


def stack_kernel(segs, hops, spectrum, mask, *refs):
    count = max(hops, 1)
    pay = refs[:count]
    small, step_table, lag, out = refs[count : count + 4]
    xs, lhs, z, near, *prod = refs[count + 4 :]
    hop = pay[0].shape[1] - LANES
    rows = mask.shape[0] // segs
    group = lax.axis_index("recv")
    me = lax.axis_index("tm")
    sources = sum(p.shape[0] for p in pay) // segs
    if hops:
        per_part = sources // 2
        for hop_no, part in enumerate(pay):
            side, sender = holder(hop_no, group // 2, group % 2, me, segs)
            for half in range(2):
                for k in range(2):
                    for i in range(per_part):
                        row = (2 * half + k) * per_part + i
                        at = (sender ^ k) * sources + (side ^ half) * per_part + i
                        xs[pl.ds(at, 1), :] = part[row : row + 1, :]
    else:
        xs[: segs * sources, :] = pay[0][...]
    xs[segs * sources :, :] = jnp.zeros((sources, hop + LANES), F32)
    count = segs * sources
    spectra(xs, count, sources, small, step_table, lhs, z)

    def put(p, x, y):
        near[p, :, :LANES] = x
        near[p, :, LANES:] = y

    whiten(z, count, 0, count, small, put)
    size = count * rows
    total = None
    for p in range(PAIRS):
        for k in range(segs):
            rx, ry = (spectrum[p, k * rows : (k + 1) * rows, c * LANES : (c + 1) * LANES] for c in range(2))
            for s in range(sources):
                i = k * sources + s
                sx, sy = (near[p, i : i + 1, c * LANES : (c + 1) * LANES] for c in range(2))
                for c, cross in enumerate((sx * rx + sy * ry, sx * ry - sy * rx)):
                    cols = slice(c * LANES, (c + 1) * LANES)
                    high, low = split(cross)
                    prod[p][i * rows : (i + 1) * rows, cols] = high
                    prod[p][size + i * rows : size + (i + 1) * rows, cols] = low
        depth = slice(2 * p * LANES, (2 * p + 2) * LANES)
        both = dot(prod[p][...], lag[0, depth, :])
        part = both[:size] + both[size:] + dot(prod[p][:size, :], lag[1, depth, :])
        total = part if total is None else total + part
    scale = lax.rsqrt(jnp.mean(total * total, axis=1, keepdims=True) + 1e-6)
    for s in range(sources):
        stack = None
        for k in range(segs):
            i = k * sources + s
            weight = mask[k * rows : (k + 1) * rows, 0:1] * xs[i : i + 1, hop : hop + 1]
            term = total[i * rows : (i + 1) * rows, :] * (weight * scale[i * rows : (i + 1) * rows, :])
            stack = term if stack is None else stack + term
        out[s] = stack


def chosen(values, index):
    if isinstance(index, int):
        return values[index]
    return sum(jnp.where(index == i, value, 0) for i, value in enumerate(values))


def holder(hop, place, side, me, segs):
    packed = chosen(ROUTES[hop], me) >> (3 * (2 * place + side))
    return packed & 1, 2 * ((packed >> 2) & 1) + ((packed >> 1) & 1)


def vmem(count):
    return [pl.BlockSpec(memory_space=pltpu.VMEM)] * count


PARAMS = dict(compiler_params=pltpu.CompilerParams(vmem_limit_bytes=32 * 1024 * 1024))


def other(value, segs, k):
    return lax.ppermute(value, "tm", [(i, i ^ k) for i in range(segs)])


def local(record, source_channels, valid_mask):
    rows, hop = record.shape
    segs = lax.axis_size("tm")
    groups = lax.axis_size("recv")
    sources = source_channels.shape[0]
    mine = sources // segs
    width = hop + LANES
    small, step_table, constant = tables(2 * hop)
    constant = pltpu.with_memory_space_constraint(constant, pltpu.HBM)
    hbm = pl.BlockSpec(memory_space=pltpu.HBM)
    fast = segs == 4 and groups == 2 * segs and sources % groups == 0
    per_group = sources // groups if fast else 0
    payload, waves, *piece = pl.pallas_call(
        functools.partial(join_kernel, per_group),
        out_shape=(
            jax.ShapeDtypeStruct((rows, width), F32),
            jax.ShapeDtypeStruct(constant.shape, F32),
            *[jax.ShapeDtypeStruct((per_group, width), F32)] * fast,
        ),
        in_specs=[hbm] * 4,
        out_specs=tuple(vmem(2 + fast)),
        scratch_shapes=[
            pltpu.VMEM((1, rows), jnp.int32),
            pltpu.SMEM((sources,), jnp.int32),
            pltpu.SemaphoreType.DMA((4,)),
        ],
        name="join",
        **PARAMS,
    )(*[pltpu.with_memory_space_constraint(a, pltpu.HBM) for a in (record, valid_mask.reshape(1, rows), source_channels)], constant)
    lag = pl.pallas_call(
        lag_kernel,
        out_shape=jax.ShapeDtypeStruct((2, RADIX * LANES, LAGS), BF),
        in_specs=vmem(1),
        out_specs=pl.BlockSpec(memory_space=pltpu.VMEM),
        name="waves",
        **PARAMS,
    )(waves)
    blocks = [payload] + [other(payload, segs, k) for k in range(1, segs)]
    if fast:
        hops = segs // 2
        pieces = [piece[0]]
        for side, bit in ((0, 1), (1, 0), (1, 1)):
            route = [(r * segs + t, (r ^ side) * segs + (t ^ bit)) for r in range(groups) for t in range(segs)]
            pieces.append(lax.ppermute(piece[0], ("recv", "tm"), route))
        pieces, lag = lax.optimization_barrier((pieces, lag))
        picked = jnp.concatenate(pieces, axis=0)
        pay = []
        for hop_no in range(hops):
            route = []
            for r in range(groups):
                for t in range(segs):
                    side, sender = holder(hop_no, r // 2, r % 2, t, segs)
                    route.append(((2 * t + side) * segs + sender, r * segs + t))
            pay.append(lax.ppermute(picked, ("recv", "tm"), route))
    else:
        hops = 0
        row = source_channels - lax.axis_index("recv") * rows
        here = (row >= 0) & (row < rows)
        mine_now = jnp.where(here[:, None], payload[jnp.clip(row, 0, rows - 1)], 0.0)
        whole = lax.psum(mine_now, "recv").reshape(segs, mine, width)
        whole = lax.all_to_all(whole, "tm", 0, 0)
        pay = [whole.reshape(segs * mine, width)]

    count = segs * rows
    spectrum, weights = pl.pallas_call(
        functools.partial(receiver_kernel, segs),
        out_shape=(
            jax.ShapeDtypeStruct((PAIRS, count, 2 * LANES), F32),
            jax.ShapeDtypeStruct((count, LANES), F32),
        ),
        in_specs=vmem(segs + 2),
        out_specs=tuple(vmem(2)),
        scratch_shapes=[
            pltpu.VMEM((count + rows, hop), F32),
            pltpu.VMEM((2 * RADIX * count, 2 * LANES), BF),
            pltpu.VMEM((RADIX * count, LANES), F32),
        ],
        name="receivers",
        **PARAMS,
    )(*blocks, small, step_table)

    src_count = segs * mine
    return pl.pallas_call(
        functools.partial(stack_kernel, segs, hops),
        out_shape=jax.ShapeDtypeStruct((mine, rows, LAGS), F32),
        in_specs=vmem(5 + len(pay)),
        out_specs=pl.BlockSpec(memory_space=pltpu.VMEM),
        scratch_shapes=[
            pltpu.VMEM((src_count + mine, width), F32),
            pltpu.VMEM((2 * RADIX * src_count, 2 * LANES), BF),
            pltpu.VMEM((RADIX * src_count, LANES), F32),
            pltpu.VMEM((PAIRS, src_count, 2 * LANES), F32),
            *[pltpu.VMEM((2 * src_count * rows, 2 * LANES), BF)] * PAIRS,
        ],
        name="stacks",
        **PARAMS,
    )(spectrum, weights, *pay, small, step_table, lag)


def solution(mesh):
    placed = (P("recv", "tm"), P(), P("recv", "tm"))
    return jax.shard_map(
        local, mesh=mesh, in_specs=placed, out_specs=P("tm", "recv", None), check_vma=False
    )
```

```python
import functools

import jax
import jax.numpy as jnp
import ml_dtypes
import numpy as np
from jax import lax
from jax.experimental import pallas as pl
from jax.experimental.pallas import tpu as pltpu
from jax.sharding import PartitionSpec as P

LANES = 128
LAGS = 256
SMOOTH = 64
RADIX = 16
PAIRS = RADIX // 2
ROUTES = ((16288538, 6472634, 2894654, 14524972), (2279102, 11640342, 15946392, 7032648))
BF = jnp.bfloat16
F32 = jnp.float32


def order():
    return np.arange(PAIRS)[:, None] + PAIRS * np.arange(2)


def halves(table):
    high = table.astype(ml_dtypes.bfloat16)
    return np.stack([high, (table - high.astype(np.float64)).astype(ml_dtypes.bfloat16)])


@functools.cache
def tables(seglen):
    bins = seglen // 2
    keep = bins // RADIX
    samples = np.arange(seglen)
    taper = (0.5 - 0.5 * np.cos(2 * np.pi * samples / seglen)).reshape(RADIX, LANES)
    n2 = np.arange(LANES)[:, None]
    angle = 2 * np.pi * ((n2 * np.arange(keep)[None, :]) % LANES) / LANES
    cos, sin = np.cos(angle), np.sin(angle)
    step = np.concatenate(list(halves(np.block([[cos, -sin], [-sin, -cos]]))), axis=1)
    angle = 2 * np.pi * (np.arange(RADIX)[:, None] * n2.T) / seglen
    f = order()[:, :, None] + RADIX * np.arange(keep)
    counts = np.minimum(f + SMOOTH, bins - 1) - np.maximum(f - SMOOTH, 0) + 1
    inverse_counts = (1.0 / counts).reshape(PAIRS, LANES)
    f2 = np.arange(keep)[:, None]
    angle_low = 2 * np.pi * ((f2 * np.arange(LANES)) % LANES) / LANES
    lags = np.arange(LAGS) - LAGS // 2
    angle_high = 2 * np.pi * np.arange(RADIX)[:, None] * lags / seglen
    factor = 2.0 / seglen
    small = [
        taper,
        np.cos(angle),
        np.sin(angle),
        inverse_counts,
        np.cos(angle_low),
        np.sin(angle_low),
        factor * np.cos(angle_high).reshape(-1, LANES),
        factor * np.sin(angle_high).reshape(-1, LANES),
    ]
    return np.concatenate(small).astype(np.float32), step


def radix_step(x):
    r = float(np.sqrt(0.5))
    c1 = float(np.cos(np.pi / 8))
    c3 = float(np.cos(3 * np.pi / 8))
    c = [None] + [x[n] + x[16 - n] for n in range(1, 8)]
    s = [None] + [x[n] - x[16 - n] for n in range(1, 8)]
    e = [x[0] + x[8]] + [c[n] + c[8 - n] for n in range(1, 4)] + [c[4]]
    o = [x[0] - x[8]] + [c[n] - c[8 - n] for n in range(1, 4)]
    g = [None] + [s[n] - s[8 - n] for n in range(1, 4)]
    h = [None] + [s[n] + s[8 - n] for n in range(1, 4)] + [s[4]]
    e04 = e[0] + e[4]
    e04m = e[0] - e[4]
    e13 = e[1] + e[3]
    e13m = r * (e[1] - e[3])
    e042 = e04 + e[2]
    g13 = r * (g[1] + g[3])
    o2 = r * o[2]
    h2 = r * h[2]
    re = {
        0: e042 + e13,
        8: e042 - e13,
        4: e04 - e[2],
        2: e04m + e13m,
        6: e04m - e13m,
        1: (o[0] + o2) + (c1 * o[1] + c3 * o[3]),
        7: (o[0] + o2) - (c1 * o[1] + c3 * o[3]),
        3: (o[0] - o2) + (c3 * o[1] - c1 * o[3]),
        5: (o[0] - o2) - (c3 * o[1] - c1 * o[3]),
    }
    im = {
        2: g13 + g[2],
        4: g[1] - g[3],
        6: g13 - g[2],
        1: (h2 + h[4]) + (c3 * h[1] + c1 * h[3]),
        7: (c3 * h[1] + c1 * h[3]) - (h2 + h[4]),
        3: (h2 - h[4]) + (c1 * h[1] - c3 * h[3]),
        5: (c1 * h[1] - c3 * h[3]) - (h2 - h[4]),
    }
    return re, im


def split(value):
    high = value.astype(BF)
    return high, (value - high.astype(F32)).astype(BF)


def dot(a, b):
    return jnp.dot(a, b, preferred_element_type=F32)


def spectra(xs, count, shift, small, step_table, lhs, z):
    seglen = RADIX * LANES
    step = 16
    every = RADIX * count

    def group(first):
        x = [xs[first : first + step, n * LANES : (n + 1) * LANES] for n in range(PAIRS)]
        x += [xs[first + shift : first + shift + step, n * LANES : (n + 1) * LANES] for n in range(PAIRS)]
        total = x[0]
        for part in x[1:]:
            total = total + part
        mean = jnp.sum(total, axis=1, keepdims=True) * (1.0 / seglen)
        x = [(x[n] - mean) * small[n : n + 1, :] for n in range(RADIX)]
        re, im = radix_step(x)
        for p in range(PAIRS):
            for half in range(2):
                f1 = p + PAIRS * half
                cos, sin = small[RADIX + f1 : RADIX + f1 + 1, :], small[2 * RADIX + f1 : 2 * RADIX + f1 + 1, :]
                if f1 == 0:
                    parts = (re[0], jnp.zeros_like(re[0]))
                elif f1 == PAIRS:
                    parts = (re[f1] * cos, re[f1] * sin)
                elif f1 < PAIRS:
                    parts = (re[f1] * cos - im[f1] * sin, re[f1] * sin + im[f1] * cos)
                else:
                    a, b = re[RADIX - f1], im[RADIX - f1]
                    parts = (a * cos + b * sin, a * sin - b * cos)
                for i, part in enumerate(parts):
                    high, low = split(part)
                    cols = slice(i * LANES, (i + 1) * LANES)
                    at = f1 * count + first
                    lhs[at : at + step, cols] = high
                    lhs[every + at : every + at + step, cols] = low

    for first in range(0, count, step):
        group(first)
    both = dot(lhs[...], step_table[...])
    both = both[:, :LANES] + both[:, LANES:]
    z[...] = both[:every] + both[every:]


def whiten(z, count, first, height, small, put):
    keep = LANES // 2
    lane = lax.broadcasted_iota(jnp.int32, (height, LANES), 1)
    place = lane % keep
    upper = lane >= keep
    blocks = []
    for p in range(PAIRS):
        a = z[p * count + first : p * count + first + height, :]
        b = z[(p + PAIRS) * count + first : (p + PAIRS) * count + first + height, :]
        blocks.append((jnp.where(upper, pltpu.roll(b, keep, 1), a), jnp.where(upper, b, pltpu.roll(a, keep, 1))))
    power = [x * x + y * y for x, y in blocks]
    upto = [power[0]]
    for p in range(1, PAIRS):
        upto.append(upto[-1] + power[p])
    since = [power[PAIRS - 1]]
    for p in range(PAIRS - 2, -1, -1):
        since.append(since[-1] + power[p])
    since = since[::-1]
    half = upto[-1]
    reach = SMOOTH // RADIX

    def moved(value, by):
        inside = (place < keep - by) if by > 0 else (place >= -by)
        return jnp.where(inside, pltpu.roll(value, -by % LANES, 1), 0.0)

    def across(by):
        if by == 0:
            return pltpu.roll(half, keep, 1)
        inside = (place < keep - by) if by > 0 else (place >= -by)
        return jnp.where(inside, pltpu.roll(half, (keep - by) % LANES, 1), 0.0)

    inner = half + across(0)
    for by in range(1, reach):
        inner = inner + ((moved(half, by) + moved(half, -by)) + (across(by) + across(-by)))
    inner = inner + (jnp.where(upper, across(reach), 0.0) + jnp.where(upper, 0.0, across(-reach)))
    for p, (x, y) in enumerate(blocks):
        window = inner + (moved(since[p], -reach) + moved(upto[p], reach))
        scale = lax.rsqrt(window * small[3 * RADIX + p : 3 * RADIX + p + 1, :] + 1e-6)
        put(p, x * scale, y * scale)


def join_kernel(per_group, record, valid, src, constant, step_constant, out, small, step_table, *refs):
    *picked, row, channels, sems = refs
    rows, hop = record.shape
    copies = [
        pltpu.make_async_copy(src, channels, sems.at[0]),
        pltpu.make_async_copy(valid, row, sems.at[1]),
        pltpu.make_async_copy(record, out.at[:, pl.ds(0, hop)], sems.at[2]),
        pltpu.make_async_copy(constant, small, sems.at[3]),
        pltpu.make_async_copy(step_constant, step_table, sems.at[4]),
    ]
    for copy in copies:
        copy.start()
    copies[1].wait()
    square = (rows, rows)
    here = lax.broadcasted_iota(jnp.int32, square, 0) == lax.broadcasted_iota(jnp.int32, square, 1)
    column = jnp.sum(jnp.where(here, row[...].astype(F32), 0.0), axis=1, keepdims=True)
    out[:, hop:] = jnp.broadcast_to(column, (rows, LANES))
    copies[0].wait()
    copies[2].wait()
    first = lax.axis_index("recv")
    for i in range(per_group):
        place = channels[first * per_group + i] - first * rows
        wanted = lax.broadcasted_iota(jnp.int32, out.shape, 0) == place
        picked[0][i : i + 1, :] = jnp.sum(jnp.where(wanted, out[...], 0.0), axis=0, keepdims=True)
    copies[3].wait()
    copies[4].wait()


def lag_kernel(small, lag):
    keep = LANES // 2
    step = 16
    low = 3 * RADIX + PAIRS
    high = low + 2 * keep
    wide = LAGS // LANES
    first = lax.broadcasted_iota(jnp.int32, (step, LANES), 0) == 0
    for f1 in range(RADIX):
        for h in range(wide):
            at = high + f1 * wide + h
            cos_high = small[at : at + 1, :]
            sin_high = small[at + RADIX * wide : at + RADIX * wide + 1, :]
            for f2 in range(0, keep, step):
                cos_low = small[low + f2 : low + f2 + step, :]
                sin_low = small[low + keep + f2 : low + keep + f2 + step, :]
                cos = cos_high * cos_low - sin_high * sin_low
                sin = sin_high * cos_low + cos_high * sin_low
                if f1 == 0 and f2 == 0:
                    cos = jnp.where(first, 0.5 * cos, cos)
                    sin = jnp.where(first, 0.5 * sin, sin)
                for c, value in enumerate((cos, -sin)):
                    row = (2 * (f1 % PAIRS) + c) * LANES + (f1 // PAIRS) * keep + f2
                    for i, part in enumerate(split(value)):
                        lag[i, row : row + step, h * LANES : (h + 1) * LANES] = part


def receiver_kernel(segs, *refs):
    blocks = refs[:segs]
    small, step_table, out, mask, xs, lhs, z = refs[segs:]
    rows, width = blocks[0].shape
    hop = width - LANES
    me = lax.axis_index("tm")
    for k, block in enumerate(blocks):
        start = pl.multiple_of((me ^ k) * rows, rows)
        xs[pl.ds(start, rows), :] = block[:, :hop]
        mask[pl.ds(start, rows), :] = block[:, hop:]
    xs[segs * rows :, :] = jnp.zeros((rows, hop), F32)
    count = segs * rows

    spectra(xs, count, rows, small, step_table, lhs, z)
    for at in range(0, count, 8):

        def put(p, x, y):
            out[p, at : at + 8, :LANES] = x
            out[p, at : at + 8, LANES:] = y

        whiten(z, count, at, 8, small, put)


def stack_kernel(segs, hops, spectrum, mask, *refs):
    count = max(hops, 1)
    pay = refs[:count]
    small, step_table, lag, out = refs[count : count + 4]
    xs, lhs, z, near, *prod = refs[count + 4 :]
    hop = pay[0].shape[1] - LANES
    rows = mask.shape[0] // segs
    group = lax.axis_index("recv")
    me = lax.axis_index("tm")
    sources = sum(p.shape[0] for p in pay) // segs
    if hops:
        per_part = sources // 2
        for hop_no, part in enumerate(pay):
            side, sender = holder(hop_no, group // 2, group % 2, me, segs)
            for half in range(2):
                for k in range(2):
                    for i in range(per_part):
                        row = (2 * half + k) * per_part + i
                        at = (sender ^ k) * sources + (side ^ half) * per_part + i
                        xs[pl.ds(at, 1), :] = part[row : row + 1, :]
    else:
        xs[: segs * sources, :] = pay[0][...]
    xs[segs * sources :, :] = jnp.zeros((xs.shape[0] - segs * sources, hop + LANES), F32)
    count = segs * sources
    spectra(xs, count, sources, small, step_table, lhs, z)

    def put(p, x, y):
        near[p, :, :LANES] = x
        near[p, :, LANES:] = y

    whiten(z, count, 0, count, small, put)
    size = count * rows
    total = None
    for p in range(PAIRS):
        for k in range(segs):
            rx, ry = (spectrum[p, k * rows : (k + 1) * rows, c * LANES : (c + 1) * LANES] for c in range(2))
            for s in range(sources):
                i = k * sources + s
                sx, sy = (near[p, i : i + 1, c * LANES : (c + 1) * LANES] for c in range(2))
                for c, cross in enumerate((sx * rx + sy * ry, sx * ry - sy * rx)):
                    cols = slice(c * LANES, (c + 1) * LANES)
                    high, low = split(cross)
                    prod[p][i * rows : (i + 1) * rows, cols] = high
                    prod[p][size + i * rows : size + (i + 1) * rows, cols] = low
        depth = slice(2 * p * LANES, (2 * p + 2) * LANES)
        both = dot(prod[p][...], lag[0, depth, :])
        part = both[:size] + both[size:] + dot(prod[p][:size, :], lag[1, depth, :])
        total = part if total is None else total + part
    scale = lax.rsqrt(jnp.mean(total * total, axis=1, keepdims=True) + 1e-6)
    for s in range(sources):
        stack = None
        for k in range(segs):
            i = k * sources + s
            weight = mask[k * rows : (k + 1) * rows, 0:1] * xs[i : i + 1, hop : hop + 1]
            term = total[i * rows : (i + 1) * rows, :] * (weight * scale[i * rows : (i + 1) * rows, :])
            stack = term if stack is None else stack + term
        out[s] = stack


def chosen(values, index):
    if isinstance(index, int):
        return values[index]
    return sum(jnp.where(index == i, value, 0) for i, value in enumerate(values))


def holder(hop, place, side, me, segs):
    packed = chosen(ROUTES[hop], me) >> (3 * (2 * place + side))
    return packed & 1, 2 * ((packed >> 2) & 1) + ((packed >> 1) & 1)


def vmem(count):
    return [pl.BlockSpec(memory_space=pltpu.VMEM)] * count


PARAMS = dict(compiler_params=pltpu.CompilerParams(vmem_limit_bytes=32 * 1024 * 1024))


def other(value, segs, k):
    return lax.ppermute(value, "tm", [(i, i ^ k) for i in range(segs)])


def local(record, source_channels, valid_mask):
    rows, hop = record.shape
    segs = lax.axis_size("tm")
    groups = lax.axis_size("recv")
    sources = source_channels.shape[0]
    mine = sources // segs
    width = hop + LANES
    constant, step_constant = [pltpu.with_memory_space_constraint(c, pltpu.HBM) for c in tables(2 * hop)]
    hbm = pl.BlockSpec(memory_space=pltpu.HBM)
    fast = segs == 4 and groups == 2 * segs and sources % groups == 0
    per_group = sources // groups if fast else 0
    payload, small, step_table, *piece = pl.pallas_call(
        functools.partial(join_kernel, per_group),
        out_shape=(
            jax.ShapeDtypeStruct((rows, width), F32),
            jax.ShapeDtypeStruct(constant.shape, F32),
            jax.ShapeDtypeStruct(step_constant.shape, BF),
            *[jax.ShapeDtypeStruct((per_group, width), F32)] * fast,
        ),
        in_specs=[hbm] * 5,
        out_specs=tuple(vmem(3 + fast)),
        scratch_shapes=[
            pltpu.VMEM((1, rows), jnp.int32),
            pltpu.SMEM((sources,), jnp.int32),
            pltpu.SemaphoreType.DMA((5,)),
        ],
        name="join",
        **PARAMS,
    )(*[pltpu.with_memory_space_constraint(a, pltpu.HBM) for a in (record, valid_mask.reshape(1, rows), source_channels)], constant, step_constant)
    lag = pl.pallas_call(
        lag_kernel,
        out_shape=jax.ShapeDtypeStruct((2, RADIX * LANES, LAGS), BF),
        in_specs=vmem(1),
        out_specs=pl.BlockSpec(memory_space=pltpu.VMEM),
        name="waves",
        **PARAMS,
    )(small)
    blocks = [payload] + [other(payload, segs, k) for k in range(1, segs)]
    if fast:
        hops = segs // 2
        pieces = [piece[0]]
        for side, bit in ((0, 1), (1, 0), (1, 1)):
            route = [(r * segs + t, (r ^ side) * segs + (t ^ bit)) for r in range(groups) for t in range(segs)]
            pieces.append(lax.ppermute(piece[0], ("recv", "tm"), route))
        pieces, lag = lax.optimization_barrier((pieces, lag))
        picked = jnp.concatenate(pieces, axis=0)
        pay = []
        for hop_no in range(hops):
            route = []
            for r in range(groups):
                for t in range(segs):
                    side, sender = holder(hop_no, r // 2, r % 2, t, segs)
                    route.append(((2 * t + side) * segs + sender, r * segs + t))
            pay.append(lax.ppermute(picked, ("recv", "tm"), route))
    else:
        hops = 0
        row = source_channels - lax.axis_index("recv") * rows
        here = (row >= 0) & (row < rows)
        mine_now = jnp.where(here[:, None], payload[jnp.clip(row, 0, rows - 1)], 0.0)
        whole = lax.psum(mine_now, "recv").reshape(segs, mine, width)
        whole = lax.all_to_all(whole, "tm", 0, 0)
        pay = [whole.reshape(segs * mine, width)]

    count = segs * rows
    spectrum, weights = pl.pallas_call(
        functools.partial(receiver_kernel, segs),
        out_shape=(
            jax.ShapeDtypeStruct((PAIRS, count, 2 * LANES), F32),
            jax.ShapeDtypeStruct((count, LANES), F32),
        ),
        in_specs=vmem(segs + 2),
        out_specs=tuple(vmem(2)),
        scratch_shapes=[
            pltpu.VMEM((count + rows, hop), F32),
            pltpu.VMEM((2 * RADIX * count, 2 * LANES), BF),
            pltpu.VMEM((RADIX * count, LANES), F32),
        ],
        name="receivers",
        **PARAMS,
    )(*blocks, small, step_table)

    src_count = segs * mine
    return pl.pallas_call(
        functools.partial(stack_kernel, segs, hops),
        out_shape=jax.ShapeDtypeStruct((mine, rows, LAGS), F32),
        in_specs=vmem(5 + len(pay)),
        out_specs=pl.BlockSpec(memory_space=pltpu.VMEM),
        scratch_shapes=[
            pltpu.VMEM((8 * pl.cdiv(src_count + mine, 8) + 8, width), F32),
            pltpu.VMEM((2 * RADIX * src_count, 2 * LANES), BF),
            pltpu.VMEM((RADIX * src_count, LANES), F32),
            pltpu.VMEM((PAIRS, src_count, 2 * LANES), F32),
            *[pltpu.VMEM((2 * src_count * rows, 2 * LANES), BF)] * PAIRS,
        ],
        name="stacks",
        **PARAMS,
    )(spectrum, weights, *pay, small, step_table, lag)


def solution(mesh):
    placed = (P("recv", "tm"), P(), P("recv", "tm"))
    return jax.shard_map(
        local, mesh=mesh, in_specs=placed, out_specs=P("tm", "recv", None), check_vma=False
    )
```

```python
import functools

import jax
import jax.numpy as jnp
import ml_dtypes
import numpy as np
from jax import lax
from jax.experimental import pallas as pl
from jax.experimental.pallas import tpu as pltpu
from jax.sharding import PartitionSpec as P

LANES = 128
LAGS = 256
SMOOTH = 64
RADIX = 16
PAIRS = RADIX // 2
ROUTES = ((16288538, 6472634, 2894654, 14524972), (2279102, 11640342, 15946392, 7032648))
BF = jnp.bfloat16
F32 = jnp.float32


def order():
    return np.arange(PAIRS)[:, None] + PAIRS * np.arange(2)


def halves(table):
    high = table.astype(ml_dtypes.bfloat16)
    return np.stack([high, (table - high.astype(np.float64)).astype(ml_dtypes.bfloat16)])


@functools.cache
def tables(seglen):
    bins = seglen // 2
    keep = bins // RADIX
    samples = np.arange(seglen)
    taper = (0.5 - 0.5 * np.cos(2 * np.pi * samples / seglen)).reshape(RADIX, LANES)
    n2 = np.arange(LANES)[:, None]
    angle = 2 * np.pi * ((n2 * np.arange(keep)[None, :]) % LANES) / LANES
    cos, sin = np.cos(angle), np.sin(angle)
    step = np.concatenate(list(halves(np.block([[cos, -sin], [-sin, -cos]]))), axis=1)
    angle = 2 * np.pi * (np.arange(RADIX)[:, None] * n2.T) / seglen
    f = order()[:, :, None] + RADIX * np.arange(keep)
    counts = np.minimum(f + SMOOTH, bins - 1) - np.maximum(f - SMOOTH, 0) + 1
    inverse_counts = (1.0 / counts).reshape(PAIRS, LANES)
    f2 = np.arange(keep)[:, None]
    angle_low = 2 * np.pi * ((f2 * np.arange(LANES)) % LANES) / LANES
    lags = np.arange(LAGS) - LAGS // 2
    angle_high = 2 * np.pi * np.arange(RADIX)[:, None] * lags / seglen
    factor = 2.0 / seglen
    small = [
        taper,
        np.cos(angle),
        np.sin(angle),
        inverse_counts,
        np.cos(angle_low),
        np.sin(angle_low),
        factor * np.cos(angle_high).reshape(-1, LANES),
        factor * np.sin(angle_high).reshape(-1, LANES),
    ]
    return np.concatenate(small).astype(np.float32), step


def radix_step(x):
    r = float(np.sqrt(0.5))
    c1 = float(np.cos(np.pi / 8))
    c3 = float(np.cos(3 * np.pi / 8))
    c = [None] + [x[n] + x[16 - n] for n in range(1, 8)]
    s = [None] + [x[n] - x[16 - n] for n in range(1, 8)]
    e = [x[0] + x[8]] + [c[n] + c[8 - n] for n in range(1, 4)] + [c[4]]
    o = [x[0] - x[8]] + [c[n] - c[8 - n] for n in range(1, 4)]
    g = [None] + [s[n] - s[8 - n] for n in range(1, 4)]
    h = [None] + [s[n] + s[8 - n] for n in range(1, 4)] + [s[4]]
    e04 = e[0] + e[4]
    e04m = e[0] - e[4]
    e13 = e[1] + e[3]
    e13m = r * (e[1] - e[3])
    e042 = e04 + e[2]
    g13 = r * (g[1] + g[3])
    o2 = r * o[2]
    h2 = r * h[2]
    re = {
        0: e042 + e13,
        8: e042 - e13,
        4: e04 - e[2],
        2: e04m + e13m,
        6: e04m - e13m,
        1: (o[0] + o2) + (c1 * o[1] + c3 * o[3]),
        7: (o[0] + o2) - (c1 * o[1] + c3 * o[3]),
        3: (o[0] - o2) + (c3 * o[1] - c1 * o[3]),
        5: (o[0] - o2) - (c3 * o[1] - c1 * o[3]),
    }
    im = {
        2: g13 + g[2],
        4: g[1] - g[3],
        6: g13 - g[2],
        1: (h2 + h[4]) + (c3 * h[1] + c1 * h[3]),
        7: (c3 * h[1] + c1 * h[3]) - (h2 + h[4]),
        3: (h2 - h[4]) + (c1 * h[1] - c3 * h[3]),
        5: (c1 * h[1] - c3 * h[3]) - (h2 - h[4]),
    }
    return re, im


def split(value):
    high = value.astype(BF)
    return high, (value - high.astype(F32)).astype(BF)


def dot(a, b):
    return jnp.dot(a, b, preferred_element_type=F32)


def spectra(xs, count, shift, small, step_table, lhs, z):
    seglen = RADIX * LANES
    step = 16
    every = RADIX * count

    def group(first):
        x = [xs[first : first + step, n * LANES : (n + 1) * LANES] for n in range(PAIRS)]
        x += [xs[first + shift : first + shift + step, n * LANES : (n + 1) * LANES] for n in range(PAIRS)]
        total = x[0]
        for part in x[1:]:
            total = total + part
        mean = jnp.sum(total, axis=1, keepdims=True) * (1.0 / seglen)
        x = [(x[n] - mean) * small[n : n + 1, :] for n in range(RADIX)]
        re, im = radix_step(x)
        for p in range(PAIRS):
            for half in range(2):
                f1 = p + PAIRS * half
                cos, sin = small[RADIX + f1 : RADIX + f1 + 1, :], small[2 * RADIX + f1 : 2 * RADIX + f1 + 1, :]
                if f1 == 0:
                    parts = (re[0], jnp.zeros_like(re[0]))
                elif f1 == PAIRS:
                    parts = (re[f1] * cos, re[f1] * sin)
                elif f1 < PAIRS:
                    parts = (re[f1] * cos - im[f1] * sin, re[f1] * sin + im[f1] * cos)
                else:
                    a, b = re[RADIX - f1], im[RADIX - f1]
                    parts = (a * cos + b * sin, a * sin - b * cos)
                for i, part in enumerate(parts):
                    high, low = split(part)
                    cols = slice(i * LANES, (i + 1) * LANES)
                    at = f1 * count + first
                    lhs[at : at + step, cols] = high
                    lhs[every + at : every + at + step, cols] = low

    for first in range(0, count, step):
        group(first)
    both = dot(lhs[...], step_table[...])
    both = both[:, :LANES] + both[:, LANES:]
    z[...] = both[:every] + both[every:]


def whiten(z, count, first, height, small, put):
    keep = LANES // 2
    lane = lax.broadcasted_iota(jnp.int32, (height, LANES), 1)
    place = lane % keep
    upper = lane >= keep
    blocks = []
    for p in range(PAIRS):
        a = z[p * count + first : p * count + first + height, :]
        b = z[(p + PAIRS) * count + first : (p + PAIRS) * count + first + height, :]
        blocks.append((jnp.where(upper, pltpu.roll(b, keep, 1), a), jnp.where(upper, b, pltpu.roll(a, keep, 1))))
    power = [x * x + y * y for x, y in blocks]
    upto = [power[0]]
    for p in range(1, PAIRS):
        upto.append(upto[-1] + power[p])
    since = [power[PAIRS - 1]]
    for p in range(PAIRS - 2, -1, -1):
        since.append(since[-1] + power[p])
    since = since[::-1]
    half = upto[-1]
    reach = SMOOTH // RADIX

    def moved(value, by):
        inside = (place < keep - by) if by > 0 else (place >= -by)
        return jnp.where(inside, pltpu.roll(value, -by % LANES, 1), 0.0)

    def across(by):
        if by == 0:
            return pltpu.roll(half, keep, 1)
        inside = (place < keep - by) if by > 0 else (place >= -by)
        return jnp.where(inside, pltpu.roll(half, (keep - by) % LANES, 1), 0.0)

    inner = half + across(0)
    for by in range(1, reach):
        inner = inner + ((moved(half, by) + moved(half, -by)) + (across(by) + across(-by)))
    inner = inner + (jnp.where(upper, across(reach), 0.0) + jnp.where(upper, 0.0, across(-reach)))
    for p, (x, y) in enumerate(blocks):
        window = inner + (moved(since[p], -reach) + moved(upto[p], reach))
        scale = lax.rsqrt(window * small[3 * RADIX + p : 3 * RADIX + p + 1, :] + 1e-6)
        put(p, x * scale, y * scale)


def join_kernel(per_group, record, valid, src, constant, step_constant, out, small, step_table, *refs):
    *picked, row, channels, sems = refs
    rows, hop = record.shape
    copies = [
        pltpu.make_async_copy(src, channels, sems.at[0]),
        pltpu.make_async_copy(valid, row, sems.at[1]),
        pltpu.make_async_copy(record, out.at[:, pl.ds(0, hop)], sems.at[2]),
        pltpu.make_async_copy(constant, small, sems.at[3]),
        pltpu.make_async_copy(step_constant, step_table, sems.at[4]),
    ]
    for i in (2, 0, 1, 3, 4):
        copies[i].start()
    copies[1].wait()
    square = (rows, rows)
    here = lax.broadcasted_iota(jnp.int32, square, 0) == lax.broadcasted_iota(jnp.int32, square, 1)
    column = jnp.sum(jnp.where(here, row[...].astype(F32), 0.0), axis=1, keepdims=True)
    out[:, hop:] = jnp.broadcast_to(column, (rows, LANES))
    copies[0].wait()
    copies[2].wait()
    first = lax.axis_index("recv")
    for i in range(per_group):
        place = channels[first * per_group + i] - first * rows
        picked[0][i : i + 1, :] = out[pl.ds(place, 1), :]
    copies[3].wait()
    copies[4].wait()


def lag_kernel(small, lag):
    keep = LANES // 2
    step = 16
    low = 3 * RADIX + PAIRS
    high = low + 2 * keep
    wide = LAGS // LANES
    first = lax.broadcasted_iota(jnp.int32, (step, LANES), 0) == 0
    for f1 in range(RADIX):
        for h in range(wide):
            at = high + f1 * wide + h
            cos_high = small[at : at + 1, :]
            sin_high = small[at + RADIX * wide : at + RADIX * wide + 1, :]
            for f2 in range(0, keep, step):
                cos_low = small[low + f2 : low + f2 + step, :]
                sin_low = small[low + keep + f2 : low + keep + f2 + step, :]
                cos = cos_high * cos_low - sin_high * sin_low
                sin = sin_high * cos_low + cos_high * sin_low
                if f1 == 0 and f2 == 0:
                    cos = jnp.where(first, 0.5 * cos, cos)
                    sin = jnp.where(first, 0.5 * sin, sin)
                for c, value in enumerate((cos, -sin)):
                    row = (2 * (f1 % PAIRS) + c) * LANES + (f1 // PAIRS) * keep + f2
                    for i, part in enumerate(split(value)):
                        lag[i, row : row + step, h * LANES : (h + 1) * LANES] = part


def receiver_kernel(segs, *refs):
    blocks = refs[:segs]
    small, step_table, out, mask, xs, lhs, z = refs[segs:]
    rows, width = blocks[0].shape
    hop = width - LANES
    me = lax.axis_index("tm")
    for k, block in enumerate(blocks):
        start = pl.multiple_of((me ^ k) * rows, rows)
        xs[pl.ds(start, rows), :] = block[:, :hop]
        mask[pl.ds(start, rows), :] = block[:, hop:]
    xs[segs * rows :, :] = jnp.zeros((rows, hop), F32)
    count = segs * rows

    spectra(xs, count, rows, small, step_table, lhs, z)
    for at in range(0, count, 16):

        def put(p, x, y):
            out[p, at : at + 16, :LANES] = x
            out[p, at : at + 16, LANES:] = y

        whiten(z, count, at, 16, small, put)


def stack_kernel(segs, hops, spectrum, mask, *refs):
    count = max(hops, 1)
    pay = refs[:count]
    small, step_table, lag, out = refs[count : count + 4]
    xs, lhs, z, near, *prod = refs[count + 4 :]
    hop = pay[0].shape[1] - LANES
    rows = mask.shape[0] // segs
    group = lax.axis_index("recv")
    me = lax.axis_index("tm")
    sources = sum(p.shape[0] for p in pay) // segs
    if hops:
        per_part = sources // 2
        for hop_no, part in enumerate(pay):
            side, sender = holder(hop_no, group // 2, group % 2, me, segs)
            for half in range(2):
                for k in range(2):
                    for i in range(per_part):
                        row = (2 * half + k) * per_part + i
                        at = (sender ^ k) * sources + (side ^ half) * per_part + i
                        xs[pl.ds(at, 1), :] = part[row : row + 1, :]
    else:
        xs[: segs * sources, :] = pay[0][...]
    xs[segs * sources :, :] = jnp.zeros((sources, hop + LANES), F32)
    count = segs * sources
    spectra(xs, count, sources, small, step_table, lhs, z)

    def put(p, x, y):
        near[p, :, :LANES] = x
        near[p, :, LANES:] = y

    whiten(z, count, 0, count, small, put)
    size = count * rows
    total = None
    for p in range(PAIRS):
        for k in range(segs):
            rx, ry = (spectrum[p, k * rows : (k + 1) * rows, c * LANES : (c + 1) * LANES] for c in range(2))
            for s in range(sources):
                i = k * sources + s
                sx, sy = (near[p, i : i + 1, c * LANES : (c + 1) * LANES] for c in range(2))
                for c, cross in enumerate((sx * rx + sy * ry, sx * ry - sy * rx)):
                    cols = slice(c * LANES, (c + 1) * LANES)
                    high, low = split(cross)
                    prod[p][i * rows : (i + 1) * rows, cols] = high
                    prod[p][size + i * rows : size + (i + 1) * rows, cols] = low
        depth = slice(2 * p * LANES, (2 * p + 2) * LANES)
        both = dot(prod[p][...], lag[0, depth, :])
        part = both[:size] + both[size:] + dot(prod[p][:size, :], lag[1, depth, :])
        total = part if total is None else total + part
    scale = lax.rsqrt(jnp.mean(total * total, axis=1, keepdims=True) + 1e-6)
    for s in range(sources):
        stack = None
        for k in range(segs):
            i = k * sources + s
            weight = mask[k * rows : (k + 1) * rows, 0:1] * xs[i : i + 1, hop : hop + 1]
            term = total[i * rows : (i + 1) * rows, :] * (weight * scale[i * rows : (i + 1) * rows, :])
            stack = term if stack is None else stack + term
        out[s] = stack


def chosen(values, index):
    if isinstance(index, int):
        return values[index]
    return sum(jnp.where(index == i, value, 0) for i, value in enumerate(values))


def holder(hop, place, side, me, segs):
    packed = chosen(ROUTES[hop], me) >> (3 * (2 * place + side))
    return packed & 1, 2 * ((packed >> 2) & 1) + ((packed >> 1) & 1)


def vmem(count):
    return [pl.BlockSpec(memory_space=pltpu.VMEM)] * count


PARAMS = dict(compiler_params=pltpu.CompilerParams(vmem_limit_bytes=32 * 1024 * 1024))


def other(value, segs, k):
    return lax.ppermute(value, "tm", [(i, i ^ k) for i in range(segs)])


def local(record, source_channels, valid_mask):
    rows, hop = record.shape
    segs = lax.axis_size("tm")
    groups = lax.axis_size("recv")
    sources = source_channels.shape[0]
    mine = sources // segs
    width = hop + LANES
    constant, step_constant = [pltpu.with_memory_space_constraint(c, pltpu.HBM) for c in tables(2 * hop)]
    hbm = pl.BlockSpec(memory_space=pltpu.HBM)
    fast = segs == 4 and groups == 2 * segs and sources % groups == 0
    per_group = sources // groups if fast else 0
    payload, small, step_table, *piece = pl.pallas_call(
        functools.partial(join_kernel, per_group),
        out_shape=(
            jax.ShapeDtypeStruct((rows, width), F32),
            jax.ShapeDtypeStruct(constant.shape, F32),
            jax.ShapeDtypeStruct(step_constant.shape, BF),
            *[jax.ShapeDtypeStruct((per_group, width), F32)] * fast,
        ),
        in_specs=[hbm] * 5,
        out_specs=tuple(vmem(3 + fast)),
        scratch_shapes=[
            pltpu.VMEM((1, rows), jnp.int32),
            pltpu.SMEM((sources,), jnp.int32),
            pltpu.SemaphoreType.DMA((5,)),
        ],
        name="join",
        **PARAMS,
    )(*[pltpu.with_memory_space_constraint(a, pltpu.HBM) for a in (record, valid_mask.reshape(1, rows), source_channels)], constant, step_constant)
    lag = pl.pallas_call(
        lag_kernel,
        out_shape=jax.ShapeDtypeStruct((2, RADIX * LANES, LAGS), BF),
        in_specs=vmem(1),
        out_specs=pl.BlockSpec(memory_space=pltpu.VMEM),
        name="waves",
        **PARAMS,
    )(small)
    blocks = [payload] + [other(payload, segs, k) for k in range(1, segs)]
    if fast:
        hops = segs // 2
        pieces = [piece[0]]
        for side, bit in ((0, 1), (1, 0), (1, 1)):
            route = [(r * segs + t, (r ^ side) * segs + (t ^ bit)) for r in range(groups) for t in range(segs)]
            pieces.append(lax.ppermute(piece[0], ("recv", "tm"), route))
        pieces, lag = lax.optimization_barrier((pieces, lag))
        picked = jnp.concatenate(pieces, axis=0)
        pay = []
        for hop_no in range(hops):
            route = []
            for r in range(groups):
                for t in range(segs):
                    side, sender = holder(hop_no, r // 2, r % 2, t, segs)
                    route.append(((2 * t + side) * segs + sender, r * segs + t))
            pay.append(lax.ppermute(picked, ("recv", "tm"), route))
    else:
        hops = 0
        row = source_channels - lax.axis_index("recv") * rows
        here = (row >= 0) & (row < rows)
        mine_now = jnp.where(here[:, None], payload[jnp.clip(row, 0, rows - 1)], 0.0)
        whole = lax.psum(mine_now, "recv").reshape(segs, mine, width)
        whole = lax.all_to_all(whole, "tm", 0, 0)
        pay = [whole.reshape(segs * mine, width)]

    count = segs * rows
    spectrum, weights = pl.pallas_call(
        functools.partial(receiver_kernel, segs),
        out_shape=(
            jax.ShapeDtypeStruct((PAIRS, count, 2 * LANES), F32),
            jax.ShapeDtypeStruct((count, LANES), F32),
        ),
        in_specs=vmem(segs + 2),
        out_specs=tuple(vmem(2)),
        scratch_shapes=[
            pltpu.VMEM((count + rows, hop), F32),
            pltpu.VMEM((2 * RADIX * count, 2 * LANES), BF),
            pltpu.VMEM((RADIX * count, LANES), F32),
        ],
        name="receivers",
        **PARAMS,
    )(*blocks, small, step_table)

    src_count = segs * mine
    return pl.pallas_call(
        functools.partial(stack_kernel, segs, hops),
        out_shape=jax.ShapeDtypeStruct((mine, rows, LAGS), F32),
        in_specs=vmem(5 + len(pay)),
        out_specs=pl.BlockSpec(memory_space=pltpu.VMEM),
        scratch_shapes=[
            pltpu.VMEM((src_count + mine, width), F32),
            pltpu.VMEM((2 * RADIX * src_count, 2 * LANES), BF),
            pltpu.VMEM((RADIX * src_count, LANES), F32),
            pltpu.VMEM((PAIRS, src_count, 2 * LANES), F32),
            *[pltpu.VMEM((2 * src_count * rows, 2 * LANES), BF)] * PAIRS,
        ],
        name="stacks",
        **PARAMS,
    )(spectrum, weights, *pay, small, step_table, lag)


def solution(mesh):
    placed = (P("recv", "tm"), P(), P("recv", "tm"))
    return jax.shard_map(
        local, mesh=mesh, in_specs=placed, out_specs=P("tm", "recv", None), check_vma=False
    )
```
